32 devices in a mesh: wall: 4 (over z), span: 4 (over y, x), stream: 2 (over core).
Axes of the slice: x: 2, y: 2, z: 4, core: 2. Of those that a mesh axis runs over, the one named last changes fastest.
Arguments:
- conserved: float32 [5, 32, 384, 512], P(None, 'stream', 'wall', 'span'), may hold values from -6 to 6
- wall_metric: float32 [32, 384, 512], P('stream', 'wall', 'span'), may hold values from 0.5 to 4
- span_metric: float32 [32, 384, 512], P('stream', 'wall', 'span'), may hold values from 0.5 to 4
Outputs:
- wall_slope: float32 [5, 32, 384, 512], P(None, 'stream', 'wall', 'span')
- span_slope: float32 [5, 32, 384, 512], P(None, 'stream', 'wall', 'span')
The draws below stay inside these ranges and needn't reach their ends.
All inputs are finite; a program needn't handle non-finite values.
Results may differ from the reference program's by a relative error of at most 0.0003.
Values sent between devices are 32-bit elements; how exact they have to be, the bound alone decides.
A program may use at most 128 MiB of HBM per device.

```python
import math
import jax
import jax.numpy as jnp
import numpy as np
from jax import lax

FIELDS = 5
PLANES = 32
NW = 384
NS = 512


def block_scale(stream_key, shape, pieces, least, largest):
    def one(axis_at, shards_of):
        heights = jax.random.uniform(jax.random.fold_in(jax.random.fold_in(stream_key, 6), axis_at), (shards_of,), jnp.float32, least / len(pieces), largest / len(pieces))
        return jnp.repeat(jnp.exp(heights), shape[axis_at] // shards_of).reshape((-1,) + (1,) * (len(shape) - axis_at - 1))

    gain = one(*pieces[0])
    for cut in pieces[1:]:
        gain = gain * one(*cut)
    return gain


def gaussian(own_key, shape, spread, limit, pieces=(), kind=jnp.bfloat16):
    level = block_scale(own_key, shape, pieces, -0.22, 0.18) if pieces else 1.0
    values = jax.random.normal(own_key, shape, jnp.float32) * spread * level
    return jnp.minimum(jnp.maximum(values, -limit), limit).astype(kind)


def setup_inputs(seed: int = 0) -> dict:
    streams_of = jax.random.split(jax.random.key(seed), 4)
    conserved = gaussian(streams_of[0], (FIELDS, PLANES, NW, NS), 1.0, 6.0, ((1, 2), (2, 4), (3, 4)), jnp.float32)
    wall_metric = jnp.clip(jnp.exp(math.log(4.0) - 2.0794415 * jax.random.uniform(streams_of[1], (PLANES, NW, NS), jnp.float32) ** block_scale(streams_of[1], (PLANES, NW, NS), ((0, 2), (1, 4), (2, 4)), -0.2, 0.2)), 0.5, 4.0)
    span_metric = jnp.clip(jnp.exp(math.log(4.0) - 2.0794415 * jax.random.uniform(streams_of[2], (PLANES, NW, NS), jnp.float32) ** block_scale(streams_of[2], (PLANES, NW, NS), ((0, 2), (1, 4), (2, 4)), -0.2, 0.2)), 0.5, 4.0)
    return dict(conserved=conserved, wall_metric=wall_metric, span_metric=span_metric)


band_alpha = 0.4995


def line_coefficients(length_all):
    lower_band = np.full(length_all, band_alpha)
    lower_band[1] = 0.25
    lower_band[length_all - 2] = 0.25
    lower_band[0] = 0.0
    lower_band[length_all - 1] = 0.0
    scales = np.zeros(length_all)
    pivots = np.zeros(length_all)
    previous = 0.0
    for row_idx in range(length_all):
        scales[row_idx] = 1.0 / (1.0 - lower_band[row_idx] * previous)
        pivots[row_idx] = lower_band[row_idx] * scales[row_idx]
        previous = pivots[row_idx]
    near_coef = (band_alpha + 2.0) / 3.0
    far_coef = (4.0 * band_alpha - 1.0) / 12.0
    weights = np.zeros((5, length_all))
    weights[:, :] = np.array([-far_coef, -near_coef, 0.0, near_coef, far_coef])[:, None]
    weights[:, 1] = [0.0, -0.75, 0.0, 0.75, 0.0]
    weights[:, length_all - 2] = [0.0, -0.75, 0.0, 0.75, 0.0]
    weights[:, 0] = [0.0, 0.0, -1.5, 2.0, -0.5]
    weights[:, length_all - 1] = [0.5, -2.0, 1.5, 0.0, 0.0]
    return lower_band, scales, pivots, weights


def line_slope(conserved, axis_pos):
    length_all = conserved.shape[axis_pos]
    lower_band, scales, pivots, weights = line_coefficients(length_all)
    line_data = jnp.moveaxis(conserved, axis_pos, 0)
    padded = jnp.pad(line_data, ((2, 2), (0, 0), (0, 0), (0, 0)))
    right_side = 0.0
    for offset in range(5):
        coefficient = jnp.asarray(weights[offset], jnp.float32)[:, None, None, None]
        right_side = right_side + coefficient * padded[offset:offset + length_all]
    band_low = jnp.asarray(lower_band, jnp.float32)
    band_scale = jnp.asarray(scales, jnp.float32)
    band_pivot = jnp.asarray(pivots, jnp.float32)

    def forward(running, row_item):
        row_value, lower_coef, scale_coef = row_item
        updated = (row_value - lower_coef * running) * scale_coef
        return updated, updated

    def backward(running, row_item):
        row_value, pivot_coef = row_item
        updated = row_value - pivot_coef * running
        return updated, updated

    start_row = jnp.zeros(line_data.shape[1:], jnp.float32)
    _, reduced = lax.scan(forward, start_row, (right_side, band_low, band_scale))
    _, slopes = lax.scan(backward, start_row, (reduced, band_pivot), reverse=True)
    return jnp.moveaxis(slopes, 0, axis_pos)


def reference(conserved, wall_metric, span_metric):
    wall_part = line_slope(conserved, 2)
    span_part = line_slope(conserved, 3)
    return wall_metric[None] * wall_part, span_metric[None] * span_part
```

```python
import functools

import jax
import jax.numpy as jnp
import ml_dtypes
import numpy as np
from jax import lax
from jax.experimental import pallas as pl
from jax.experimental.pallas import tpu as pltpu
from jax.sharding import PartitionSpec as P

band_alpha = 0.4995
MESH = pl.DeviceIdType.MESH


def line_operators(length_all):
    lower_band = np.full(length_all, band_alpha)
    lower_band[[1, length_all - 2]] = 0.25
    lower_band[[0, length_all - 1]] = 0.0
    band = np.eye(length_all)
    rows = np.arange(length_all)
    band[rows[1:], rows[:-1]] = lower_band[1:]
    band[rows[:-1], rows[1:]] = lower_band[:-1]
    near_coef = (band_alpha + 2.0) / 3.0
    far_coef = (4.0 * band_alpha - 1.0) / 12.0
    weights = np.zeros((5, length_all))
    weights[:, :] = np.array([-far_coef, -near_coef, 0.0, near_coef, far_coef])[:, None]
    weights[:, 1] = [0.0, -0.75, 0.0, 0.75, 0.0]
    weights[:, length_all - 2] = [0.0, -0.75, 0.0, 0.75, 0.0]
    weights[:, 0] = [0.0, 0.0, -1.5, 2.0, -0.5]
    weights[:, length_all - 1] = [0.5, -2.0, 1.5, 0.0, 0.0]
    right = np.zeros((length_all, length_all))
    for offset in range(-2, 3):
        good = rows[(rows + offset >= 0) & (rows + offset < length_all)]
        right[good, good + offset] = weights[offset + 2, good]
    inverse = np.linalg.inv(band)
    return inverse, inverse @ right


def block_tables(pieces, block):
    inverse, whole = line_operators(pieces * block)
    own = np.zeros((pieces, block, block))
    fix = np.zeros((pieces, block, 8))
    sends = np.zeros((pieces, 8, block))
    gains = np.zeros((2, pieces, max(pieces - 1, 1)))
    half = block // 2
    for p in range(pieces):
        lo, hi = p * block, (p + 1) * block
        own[p] = whole[lo:hi, lo:hi]
        sends[p, 1, block - 2] = sends[p, 2, block - 1] = 1.0
        sends[p, 4, 0] = sends[p, 5, 1] = 1.0
        if p + 1 < pieces:
            shape = inverse[hi : hi + block, hi - 1] / inverse[hi, hi - 1]
            sends[p, 0] = whole[hi + half, lo:hi] / shape[half]
            fix[p + 1, :, 0] = shape
            near = whole[hi : hi + block, hi - 2 : hi]
            fix[p + 1, :, 1:3] = near - shape[:, None] * sends[p, 0, block - 2 :]
            for d in range(1, pieces - p):
                gains[0, p + d, d - 1] = inverse[lo + d * block, hi - 1] / inverse[hi, hi - 1]
        if p > 0:
            shape = inverse[lo - block : lo, lo] / inverse[lo - 1, lo]
            sends[p, 3] = whole[lo - block + half, lo:hi] / shape[half]
            fix[p - 1, :, 3] = shape
            near = whole[lo - block : lo, lo : lo + 2]
            fix[p - 1, :, 4:6] = near - shape[:, None] * sends[p, 3, :2]
            for d in range(1, p + 1):
                gains[1, p - d, d - 1] = inverse[hi - 1 - d * block, lo] / inverse[lo - 1, lo]
    return own, fix, sends, gains


def split(table):
    high = table.astype(ml_dtypes.bfloat16)
    low = (table - high.astype(np.float64)).astype(ml_dtypes.bfloat16)
    return high, low


def halves(values):
    high = values.astype(jnp.bfloat16)
    low = (values - high.astype(jnp.float32)).astype(jnp.bfloat16)
    return high, low


def exchange_kernel(
    wall_n, span_n,
    f_hbm, wall_sends, span_sends, gains, wall_tab, span_tab, span_fix,
    wall_msg, span_msg, wall_mine, span_mine, fix_mine,
    f_buf, wall_v, span_v, wall_out, span_out, wall_near, span_near, wall_far, span_far,
    load_sems, table_sems, send_sems, recv_sems,
):
    me_w, me_s, me_c = (lax.axis_index(name) for name in ("wall", "span", "stream"))
    fields, planes, rows, columns = f_buf.shape
    loads = [pltpu.make_async_copy(f_hbm.at[k], f_buf.at[k], load_sems.at[k]) for k in range(fields)]
    tables = [
        pltpu.make_async_copy(src, dst, table_sems.at[k])
        for k, (src, dst) in enumerate((
            (wall_sends.at[me_w], wall_v), (span_sends.at[me_s], span_v),
            (wall_tab.at[me_w], wall_mine), (span_tab.at[me_s], span_mine),
            (span_fix.at[me_s], fix_mine),
        ))
    ]
    for copy in tables[:2] + loads + tables[2:]:
        copy.start()

    def device(axis, shift):
        if axis == 0:
            return (me_w + shift, me_s, me_c)
        return (me_w, me_s + shift, me_c)

    axes = ((0, me_w, wall_n), (1, me_s, span_n))
    barrier = pltpu.get_barrier_semaphore()
    for axis, me, n in axes:
        for d in range(1, n):
            @pl.when(me + d < n)
            def _():
                pl.semaphore_signal(barrier, inc=1, device_id=device(axis, d), device_id_type=MESH)

            @pl.when(me >= d)
            def _():
                pl.semaphore_signal(barrier, inc=1, device_id=device(axis, -d), device_id_type=MESH)

    wall_msg[...] = jnp.zeros_like(wall_msg)
    span_msg[...] = jnp.zeros_like(span_msg)
    outs, nears, fars = (wall_out, span_out), (wall_near, span_near), (wall_far, span_far)

    def transfer(axis, side, d):
        if d == 1:
            src, dst = outs[axis].at[pl.ds(3 * side, 3)], nears[axis].at[side]
        else:
            src, dst = outs[axis].at[3 * side], fars[axis].at[side, d - 2]
        return pltpu.make_async_remote_copy(
            src_ref=src, dst_ref=dst,
            send_sem=send_sems.at[axis, side, d - 1], recv_sem=recv_sems.at[axis, side, d - 1],
            device_id=device(axis, d if side == 0 else -d), device_id_type=MESH,
        )

    def has_target(me, n, side, d):
        return me + d < n if side == 0 else me >= d

    def has_source(me, n, side, d):
        return me >= d if side == 0 else me + d < n

    def send_all(axis, me, n):
        for d in range(n - 1, 0, -1):
            for side in range(2):
                @pl.when(has_target(me, n, side, d))
                def _():
                    transfer(axis, side, d).start()

    tables[0].wait()
    for k in range(fields):
        loads[k].wait()
        here = pl.ds(k * planes, planes)
        values = f_buf[k]
        wall_out[0, here, :] = jnp.sum(values * wall_v[0][None], axis=1)
        wall_out[3, here, :] = jnp.sum(values * wall_v[1][None], axis=1)
        wall_out[1, here, :] = f_buf[k, :, rows - 2, :]
        wall_out[2, here, :] = f_buf[k, :, rows - 1, :]
        wall_out[4, here, :] = f_buf[k, :, 0, :]
        wall_out[5, here, :] = f_buf[k, :, 1, :]
    pl.semaphore_wait(barrier, wall_n + span_n - 2)
    send_all(*axes[0])

    tables[1].wait()
    tiles = planes * rows // 128
    for k in range(fields):
        high, low = halves(f_buf[k].reshape(planes * rows, columns))
        both = jnp.concatenate([high, low], axis=1)
        picked = lax.dot_general(
            span_v[...], both, (((1,), (1,)), ((), ())), preferred_element_type=jnp.float32
        )
        picked = picked[:8] + picked[8:]
        for t in range(tiles):
            for m in range(6):
                span_out[m, k * tiles + t : k * tiles + t + 1, :] = picked[m : m + 1, t * 128 : (t + 1) * 128]
    send_all(*axes[1])

    msgs = (wall_msg, span_msg)
    for axis, me, n in axes:
        for d in range(1, n):
            for side in range(2):
                @pl.when(has_source(me, n, side, d))
                def _():
                    transfer(axis, side, d).wait_recv()
                    gain = gains[axis, side, me, d - 1]
                    if d == 1:
                        msgs[axis][3 * side] += gain * nears[axis][side, 0]
                        msgs[axis][3 * side + 1] = nears[axis][side, 1]
                        msgs[axis][3 * side + 2] = nears[axis][side, 2]
                    else:
                        msgs[axis][3 * side] += gain * fars[axis][side, d - 2]
    for axis, me, n in axes:
        for d in range(1, n):
            for side in range(2):
                @pl.when(has_target(me, n, side, d))
                def _():
                    transfer(axis, side, d).wait_send()
    for copy in tables[2:]:
        copy.wait()


def slope_kernel(f_ref, wall_metric, span_metric, wall_msg, span_msg, wall_tab, span_tab, fix_tab, wall_ref, span_ref):
    fields, planes, rows, columns = f_ref.shape
    step = pl.program_id(0)
    steps = pl.num_programs(0)
    tiles = planes * rows // 128
    for k in range(fields):
        high, low = halves(f_ref[k])
        both = jnp.concatenate([high, low], axis=2).reshape(planes * rows, 2 * columns)
        spread = jnp.dot(both, span_tab[...], preferred_element_type=jnp.float32)
        first = (k * steps + step) * tiles
        edge = jnp.concatenate([span_msg[:, first + t, :] for t in range(tiles)], axis=1)
        edge_high, edge_low = halves(edge)
        edges = jnp.concatenate([edge_high.astype(jnp.float32), edge_low.astype(jnp.float32)], axis=0).T
        spread += jnp.dot(edges.astype(jnp.bfloat16), fix_tab[...], preferred_element_type=jnp.float32)
        spread = spread[:, :columns] + spread[:, columns:]
        span_ref[k] = spread.reshape(planes, rows, columns) * span_metric[...]
        for q in range(0, planes, 2):
            parts = []
            for j in (q, q + 1):
                msg_high, msg_low = halves(wall_msg[:, (k * steps + step) * planes + j, :])
                parts.append(jnp.concatenate(
                    [high[j], low[j], jnp.concatenate([msg_high, msg_low], axis=0)], axis=0
                ))
            pair = jnp.concatenate(parts, axis=1)
            solved = jnp.dot(wall_tab[...], pair, preferred_element_type=jnp.float32)
            solved = solved[:rows] + solved[rows:]
            wall_ref[k, q] = solved[:, :columns] * wall_metric[q]
            wall_ref[k, q + 1] = solved[:, columns:] * wall_metric[q + 1]


def per_device(wall_n, span_n, conserved, wall_metric, span_metric):
    fields, planes, rows, columns = conserved.shape
    slabs = fields * planes
    lines = slabs * rows // 128
    own_w, fix_w, sends_w, gains_w = block_tables(wall_n, rows)
    own_s, fix_s, sends_s, gains_s = block_tables(span_n, columns)
    bf16 = jnp.bfloat16

    wall_sends = np.broadcast_to(sends_w[:, (0, 3), :, None], (wall_n, 2, rows, 128)).astype(np.float32)
    high, low = split(sends_s)
    span_sends = np.concatenate([np.concatenate([t, t], axis=2) for t in (high, low)], axis=1)
    most = max(wall_n, span_n)
    gains = np.zeros((2, 2, most, most), np.float32)
    gains[0, :, :wall_n, : gains_w.shape[2]] = gains_w
    gains[1, :, :span_n, : gains_s.shape[2]] = gains_s
    own_high, own_low = split(own_w)
    fix_high, fix_low = split(fix_w)
    wall_tab = np.concatenate([
        np.concatenate([own_high, own_high, fix_high, fix_high], axis=2),
        np.concatenate([own_low, own_low, fix_low, fix_low], axis=2),
    ], axis=1)
    own_high, own_low = split(own_s.transpose(0, 2, 1))
    span_tab = np.concatenate([np.concatenate([own_high, own_low], axis=2)] * 2, axis=1)
    fix_high, fix_low = split(fix_s.transpose(0, 2, 1))
    span_fix = np.concatenate([np.concatenate([fix_high, fix_low], axis=2)] * 2, axis=1)

    vmem = pl.BlockSpec(memory_space=pltpu.VMEM)
    anywhere = pl.BlockSpec(memory_space=pl.ANY)
    far = max(wall_n, span_n) - 1
    wall_msg, span_msg, wall_mine, span_mine, fix_mine = pl.pallas_call(
        functools.partial(exchange_kernel, wall_n, span_n),
        out_shape=(
            jax.ShapeDtypeStruct((8, slabs, 128), jnp.float32),
            jax.ShapeDtypeStruct((8, lines, 128), jnp.float32),
            jax.ShapeDtypeStruct(wall_tab.shape[1:], bf16),
            jax.ShapeDtypeStruct(span_tab.shape[1:], bf16),
            jax.ShapeDtypeStruct(span_fix.shape[1:], bf16),
        ),
        in_specs=[anywhere, anywhere, anywhere, pl.BlockSpec(memory_space=pltpu.SMEM), anywhere, anywhere, anywhere],
        out_specs=(vmem, vmem, anywhere, anywhere, anywhere),
        scratch_shapes=[
            pltpu.VMEM(conserved.shape, jnp.float32),
            pltpu.VMEM(wall_sends.shape[1:], jnp.float32),
            pltpu.VMEM(span_sends.shape[1:], bf16),
            pltpu.VMEM((6, slabs, 128), jnp.float32),
            pltpu.VMEM((6, lines, 128), jnp.float32),
            pltpu.VMEM((2, 3, slabs, 128), jnp.float32),
            pltpu.VMEM((2, 3, lines, 128), jnp.float32),
            pltpu.VMEM((2, max(wall_n - 2, 1), slabs, 128), jnp.float32),
            pltpu.VMEM((2, max(span_n - 2, 1), lines, 128), jnp.float32),
            pltpu.SemaphoreType.DMA((fields,)),
            pltpu.SemaphoreType.DMA((5,)),
            pltpu.SemaphoreType.DMA((2, 2, far)),
            pltpu.SemaphoreType.DMA((2, 2, far)),
        ],
        compiler_params=pltpu.CompilerParams(
            collective_id=0, has_side_effects=True, vmem_limit_bytes=40 * 1024 * 1024
        ),
        name="exchange",
    )(
        conserved, jnp.asarray(wall_sends), jnp.asarray(span_sends), jnp.asarray(gains),
        jnp.asarray(wall_tab), jnp.asarray(span_tab), jnp.asarray(span_fix),
    )

    step_planes = 4
    steps = planes // step_planes
    fields_block = pl.BlockSpec((fields, step_planes, rows, columns), lambda i: (0, i, 0, 0))
    metric_block = pl.BlockSpec((step_planes, rows, columns), lambda i: (i, 0, 0))
    whole = lambda array: pl.BlockSpec(array.shape, lambda i: (0,) * array.ndim)
    flops = 2 * slabs * (rows * 256 * 256 + 192 * 256 * 128)
    return pl.pallas_call(
        slope_kernel,
        grid=(steps,),
        out_shape=(jax.ShapeDtypeStruct(conserved.shape, jnp.float32),) * 2,
        in_specs=[fields_block, metric_block, metric_block]
        + [whole(t) for t in (wall_msg, span_msg, wall_mine, span_mine, fix_mine)],
        out_specs=(fields_block, fields_block),
        compiler_params=pltpu.CompilerParams(vmem_limit_bytes=40 * 1024 * 1024),
        cost_estimate=pl.CostEstimate(flops=flops, bytes_accessed=17 * conserved.size, transcendentals=0),
        name="slopes",
    )(conserved, wall_metric, span_metric, wall_msg, span_msg, wall_mine, span_mine, fix_mine)


def solution(mesh):
    in_specs = (
        P(None, "stream", "wall", "span"),
        P("stream", "wall", "span"),
        P("stream", "wall", "span"),
    )
    out_specs = (P(None, "stream", "wall", "span"), P(None, "stream", "wall", "span"))
    sizes = (mesh.shape["wall"], mesh.shape["span"])
    return jax.shard_map(
        functools.partial(per_device, *sizes), mesh=mesh, in_specs=in_specs, out_specs=out_specs, check_vma=False
    )
```

```python
import functools

import jax
import jax.numpy as jnp
import ml_dtypes
import numpy as np
from jax import lax
from jax.experimental import pallas as pl
from jax.experimental.pallas import tpu as pltpu
from jax.sharding import PartitionSpec as P

band_alpha = 0.4995
MESH = pl.DeviceIdType.MESH


def line_operators(length_all):
    lower_band = np.full(length_all, band_alpha)
    lower_band[[1, length_all - 2]] = 0.25
    lower_band[[0, length_all - 1]] = 0.0
    band = np.eye(length_all)
    rows = np.arange(length_all)
    band[rows[1:], rows[:-1]] = lower_band[1:]
    band[rows[:-1], rows[1:]] = lower_band[:-1]
    near_coef = (band_alpha + 2.0) / 3.0
    far_coef = (4.0 * band_alpha - 1.0) / 12.0
    weights = np.zeros((5, length_all))
    weights[:, :] = np.array([-far_coef, -near_coef, 0.0, near_coef, far_coef])[:, None]
    weights[:, 1] = [0.0, -0.75, 0.0, 0.75, 0.0]
    weights[:, length_all - 2] = [0.0, -0.75, 0.0, 0.75, 0.0]
    weights[:, 0] = [0.0, 0.0, -1.5, 2.0, -0.5]
    weights[:, length_all - 1] = [0.5, -2.0, 1.5, 0.0, 0.0]
    right = np.zeros((length_all, length_all))
    for offset in range(-2, 3):
        good = rows[(rows + offset >= 0) & (rows + offset < length_all)]
        right[good, good + offset] = weights[offset + 2, good]
    inverse = np.linalg.inv(band)
    return inverse, inverse @ right


def block_tables(pieces, block):
    inverse, whole = line_operators(pieces * block)
    own = np.zeros((pieces, block, block))
    fix = np.zeros((pieces, block, 8))
    sends = np.zeros((pieces, 8, block))
    gains = np.zeros((2, pieces, max(pieces - 1, 1)))
    half = block // 2
    for p in range(pieces):
        lo, hi = p * block, (p + 1) * block
        own[p] = whole[lo:hi, lo:hi]
        sends[p, 1, block - 2] = sends[p, 2, block - 1] = 1.0
        sends[p, 4, 0] = sends[p, 5, 1] = 1.0
        if p + 1 < pieces:
            shape = inverse[hi : hi + block, hi - 1] / inverse[hi, hi - 1]
            sends[p, 0] = whole[hi + half, lo:hi] / shape[half]
            fix[p + 1, :, 0] = shape
            near = whole[hi : hi + block, hi - 2 : hi]
            fix[p + 1, :, 1:3] = near - shape[:, None] * sends[p, 0, block - 2 :]
            for d in range(1, pieces - p):
                gains[0, p + d, d - 1] = inverse[lo + d * block, hi - 1] / inverse[hi, hi - 1]
        if p > 0:
            shape = inverse[lo - block : lo, lo] / inverse[lo - 1, lo]
            sends[p, 3] = whole[lo - block + half, lo:hi] / shape[half]
            fix[p - 1, :, 3] = shape
            near = whole[lo - block : lo, lo : lo + 2]
            fix[p - 1, :, 4:6] = near - shape[:, None] * sends[p, 3, :2]
            for d in range(1, p + 1):
                gains[1, p - d, d - 1] = inverse[hi - 1 - d * block, lo] / inverse[lo - 1, lo]
    return own, fix, sends, gains


def split(table):
    high = table.astype(ml_dtypes.bfloat16)
    low = (table - high.astype(np.float64)).astype(ml_dtypes.bfloat16)
    return high, low


def halves(values):
    high = values.astype(jnp.bfloat16)
    low = (values - high.astype(jnp.float32)).astype(jnp.bfloat16)
    return high, low


def exchange_kernel(
    wall_n, span_n, wall_gains, span_gains,
    f_hbm, wall_tab, span_tab,
    wall_loc, span_loc, wall_msg, span_msg, wall_fix, span_fix,
    f_buf, wall_t, span_t, wall_out, span_out, wall_near, span_near, wall_far, span_far,
    load_sems, table_sems, send_sems, recv_sems,
):
    me_w, me_s, me_c = (lax.axis_index(name) for name in ("wall", "span", "stream"))
    fields, planes, rows, columns = f_hbm.shape
    slabs = fields * planes
    loads = [
        pltpu.make_async_copy(f_hbm.at[k], f_buf.at[pl.ds(k * planes, planes)], load_sems.at[k])
        for k in range(fields)
    ]
    tables = [
        pltpu.make_async_copy(src, dst, table_sems.at[k])
        for k, (src, dst) in enumerate((
            (wall_tab.at[me_w], wall_t), (span_tab.at[me_s], span_t),
        ))
    ]
    for copy in tables[:1] + loads[:2] + tables[1:] + loads[2:]:
        copy.start()

    def device(axis, shift):
        if axis == 0:
            return (me_w + shift, me_s, me_c)
        return (me_w, me_s + shift, me_c)

    axes = ((0, me_w, wall_n), (1, me_s, span_n))
    barrier = pltpu.get_barrier_semaphore()
    for axis, me, n in axes:
        for d in range(1, n):
            @pl.when(me + d < n)
            def _():
                pl.semaphore_signal(barrier, inc=1, device_id=device(axis, d), device_id_type=MESH)

            @pl.when(me >= d)
            def _():
                pl.semaphore_signal(barrier, inc=1, device_id=device(axis, -d), device_id_type=MESH)

    wall_msg[...] = jnp.zeros_like(wall_msg)
    span_msg[...] = jnp.zeros_like(span_msg)
    outs, nears, fars = (wall_out, span_out), (wall_near, span_near), (wall_far, span_far)
    gains = (wall_gains, span_gains)

    def transfer(axis, side, d):
        if d == 1:
            src, dst = outs[axis].at[pl.ds(3 * side, 3)], nears[axis].at[side]
        else:
            src, dst = outs[axis].at[3 * side], fars[axis].at[side, d - 2]
        return pltpu.make_async_remote_copy(
            src_ref=src, dst_ref=dst,
            send_sem=send_sems.at[axis, side, d - 1], recv_sem=recv_sems.at[axis, side, d - 1],
            device_id=device(axis, d if side == 0 else -d), device_id_type=MESH,
        )

    def has_target(me, n, side, d):
        return me + d < n if side == 0 else me >= d

    def has_source(me, n, side, d):
        return me >= d if side == 0 else me + d < n

    def send_all(axis, me, n):
        for d in range(n - 1, 0, -1):
            for side in range(2):
                @pl.when(has_target(me, n, side, d))
                def _():
                    transfer(axis, side, d).start()

    tables[0].wait()
    columns_at = 2 * rows + 16
    picks = wall_t[:rows, columns_at : columns_at + 4].astype(jnp.float32)
    picks = picks[:, :2] + picks[:, 2:]
    wall_a = jnp.broadcast_to(picks[:, 0:1], (rows, columns))
    wall_b = jnp.broadcast_to(picks[:, 1:2], (rows, columns))
    for k in range(fields):
        loads[k].wait()
        here = pl.ds(k * planes, planes)
        values = f_buf[here]
        wall_out[0, here, :] = jnp.sum(values * wall_a[None], axis=1)
        wall_out[3, here, :] = jnp.sum(values * wall_b[None], axis=1)
        wall_out[1, here, :] = f_buf[here, rows - 2, :]
        wall_out[2, here, :] = f_buf[here, rows - 1, :]
        wall_out[4, here, :] = f_buf[here, 0, :]
        wall_out[5, here, :] = f_buf[here, 1, :]
    pl.semaphore_wait(barrier, wall_n + span_n - 2)
    send_all(*axes[0])

    tables[1].wait()
    tiles = planes * rows // 128
    depth = 2 * columns
    for k in range(fields):
        high, low = halves(f_buf[pl.ds(k * planes, planes)].reshape(planes * rows, columns))
        both = jnp.concatenate([high, low], axis=1)
        picked = lax.dot_general(
            span_t[depth : depth + 16], both, (((1,), (1,)), ((), ())), preferred_element_type=jnp.float32
        )
        picked = picked[:8] + picked[8:]
        for t in range(tiles):
            for m in range(6):
                span_out[m, k * tiles + t : k * tiles + t + 1, :] = picked[m : m + 1, t * 128 : (t + 1) * 128]
    send_all(*axes[1])

    wall_fix[...] = wall_t[:, 2 * rows : 2 * rows + 16]
    span_fix[...] = span_t[depth + 16 : depth + 32]
    group = 4

    @pl.loop(0, slabs // group)
    def _(step):
        here = pl.ds(step * group, group)
        high, low = halves(f_buf[here])
        both = jnp.concatenate([high, low], axis=2).reshape(group * rows, depth)
        spread = jnp.dot(both, span_t[:depth], preferred_element_type=jnp.float32)
        spread = spread[:, :columns] + spread[:, columns:]
        span_loc[here] = spread.reshape(group, rows, columns)
        for q in range(0, group, 2):
            pair = jnp.concatenate(
                [jnp.concatenate([high[j], low[j]], axis=0) for j in (q, q + 1)], axis=1
            )
            solved = jnp.dot(wall_t[:, : 2 * rows], pair, preferred_element_type=jnp.float32)
            solved = solved[:rows] + solved[rows:]
            wall_loc[step * group + q] = solved[:, :columns]
            wall_loc[step * group + q + 1] = solved[:, columns:]

    msgs = (wall_msg, span_msg)
    for axis, me, n in axes:
        for d in range(1, n):
            for side in range(2):
                @pl.when(has_source(me, n, side, d))
                def _():
                    transfer(axis, side, d).wait_recv()
                    gain = jnp.float32(0.0)
                    for p in range(n):
                        gain = jnp.where(me == p, jnp.float32(gains[axis][side, p, d - 1]), gain)
                    if d == 1:
                        msgs[axis][3 * side] += gain * nears[axis][side, 0]
                        msgs[axis][3 * side + 1] = nears[axis][side, 1]
                        msgs[axis][3 * side + 2] = nears[axis][side, 2]
                    else:
                        msgs[axis][3 * side] += gain * fars[axis][side, d - 2]
    for axis, me, n in axes:
        for d in range(1, n):
            for side in range(2):
                @pl.when(has_target(me, n, side, d))
                def _():
                    transfer(axis, side, d).wait_send()


def correct_kernel(
    group, wall_loc, span_loc, wall_metric, span_metric, wall_msg, span_msg, wall_fix, span_fix,
    wall_hbm, span_hbm, wall_buf, span_buf, sems,
):
    planes = wall_metric.shape[0]
    slabs, rows, columns = wall_loc.shape
    tiles = group * rows // 128
    parts = planes // group

    def copies(step):
        here = pl.ds(step * group, group)
        return (
            pltpu.make_async_copy(wall_buf.at[here], wall_hbm.at[here], sems.at[0, step]),
            pltpu.make_async_copy(span_buf.at[here], span_hbm.at[here], sems.at[1, step]),
        )

    @pl.loop(0, slabs // group)
    def _(step):
        here = pl.ds(step * group, group)
        plane = (step % parts) * group
        edge = jnp.concatenate([span_msg[:, step * tiles + t, :] for t in range(tiles)], axis=1)
        edge_high, edge_low = halves(edge)
        edges = jnp.concatenate([edge_high.astype(jnp.float32), edge_low.astype(jnp.float32)], axis=0).T
        spread = jnp.dot(edges.astype(jnp.bfloat16), span_fix[...], preferred_element_type=jnp.float32)
        spread = (spread[:, :columns] + spread[:, columns:]).reshape(group, rows, columns)
        span_buf[here] = (span_loc[here] + spread) * span_metric[pl.ds(plane, group)]
        for q in range(0, group, 2):
            msgs = [
                jnp.concatenate(halves(wall_msg[:, step * group + j, :]), axis=0) for j in (q, q + 1)
            ]
            solved = jnp.dot(wall_fix[...], jnp.concatenate(msgs, axis=1), preferred_element_type=jnp.float32)
            solved = solved[:rows] + solved[rows:]
            for j in range(2):
                wall_buf[step * group + q + j] = (
                    wall_loc[step * group + q + j] + solved[:, j * columns : (j + 1) * columns]
                ) * wall_metric[plane + q + j]
        for copy in copies(step):
            copy.start()

    @pl.loop(0, slabs // group)
    def _(step):
        for copy in copies(step):
            copy.wait()


def per_device(wall_n, span_n, conserved, wall_metric, span_metric):
    fields, planes, rows, columns = conserved.shape
    slabs = fields * planes
    lines = slabs * rows // 128
    own_w, fix_w, sends_w, gains_w = block_tables(wall_n, rows)
    own_s, fix_s, sends_s, gains_s = block_tables(span_n, columns)
    f32, bf16 = jnp.float32, jnp.bfloat16

    own_high, own_low = split(own_w)
    fix_high, fix_low = split(fix_w)
    picks = np.concatenate(split(sends_w[:, (0, 3)].transpose(0, 2, 1)), axis=2)
    wall_tab = np.concatenate([
        np.concatenate([own_high, own_high, fix_high, fix_high, picks], axis=2),
        np.concatenate([own_low, own_low, fix_low, fix_low, picks], axis=2),
    ], axis=1)
    own_high, own_low = split(own_s.transpose(0, 2, 1))
    sends_high, sends_low = split(sends_s)
    fix_high, fix_low = split(fix_s.transpose(0, 2, 1))
    span_tab = np.concatenate(
        [np.concatenate([own_high, own_low], axis=2)] * 2
        + [np.concatenate([t, t], axis=2) for t in (sends_high, sends_low)]
        + [np.concatenate([fix_high, fix_low], axis=2)] * 2,
        axis=1,
    )

    vmem = pl.BlockSpec(memory_space=pltpu.VMEM)
    hbm = pl.BlockSpec(memory_space=pltpu.HBM)
    far = max(wall_n, span_n) - 1
    flat = (slabs, rows, columns)
    local = pl.pallas_call(
        functools.partial(exchange_kernel, wall_n, span_n, gains_w, gains_s),
        out_shape=(
            jax.ShapeDtypeStruct(flat, f32),
            jax.ShapeDtypeStruct(flat, f32),
            jax.ShapeDtypeStruct((8, slabs, 128), f32),
            jax.ShapeDtypeStruct((8, lines, 128), f32),
            jax.ShapeDtypeStruct((2 * rows, 16), bf16),
            jax.ShapeDtypeStruct((16, 2 * columns), bf16),
        ),
        in_specs=[hbm] * 3,
        out_specs=(vmem,) * 6,
        scratch_shapes=[
            pltpu.VMEM(flat, f32),
            pltpu.VMEM(wall_tab.shape[1:], bf16),
            pltpu.VMEM(span_tab.shape[1:], bf16),
            pltpu.VMEM((6, slabs, 128), f32),
            pltpu.VMEM((6, lines, 128), f32),
            pltpu.VMEM((2, 3, slabs, 128), f32),
            pltpu.VMEM((2, 3, lines, 128), f32),
            pltpu.VMEM((2, max(wall_n - 2, 1), slabs, 128), f32),
            pltpu.VMEM((2, max(span_n - 2, 1), lines, 128), f32),
            pltpu.SemaphoreType.DMA((fields,)),
            pltpu.SemaphoreType.DMA((2,)),
            pltpu.SemaphoreType.DMA((2, 2, far)),
            pltpu.SemaphoreType.DMA((2, 2, far)),
        ],
        compiler_params=pltpu.CompilerParams(
            collective_id=0, has_side_effects=True, vmem_limit_bytes=43 * 1024 * 1024
        ),
        name="exchange",
    )(conserved, jnp.asarray(wall_tab), jnp.asarray(span_tab))

    group = 4
    outs = pl.pallas_call(
        functools.partial(correct_kernel, group),
        out_shape=(jax.ShapeDtypeStruct(flat, f32),) * 2,
        in_specs=[vmem] * 8,
        out_specs=(hbm, hbm),
        scratch_shapes=[
            pltpu.VMEM(flat, f32), pltpu.VMEM(flat, f32), pltpu.SemaphoreType.DMA((2, slabs // group)),
        ],
        compiler_params=pltpu.CompilerParams(vmem_limit_bytes=24 * 1024 * 1024),
        cost_estimate=pl.CostEstimate(
            flops=2 * slabs * rows * columns * 16 * 8, bytes_accessed=8 * conserved.size, transcendentals=0
        ),
        name="correct",
    )(local[0], local[1], wall_metric, span_metric, *local[2:])
    return tuple(out.reshape(conserved.shape) for out in outs)


def solution(mesh):
    in_specs = (
        P(None, "stream", "wall", "span"),
        P("stream", "wall", "span"),
        P("stream", "wall", "span"),
    )
    out_specs = (P(None, "stream", "wall", "span"), P(None, "stream", "wall", "span"))
    sizes = (mesh.shape["wall"], mesh.shape["span"])
    return jax.shard_map(
        functools.partial(per_device, *sizes), mesh=mesh, in_specs=in_specs, out_specs=out_specs, check_vma=False
    )
```

```python
import functools

import jax
import jax.numpy as jnp
import ml_dtypes
import numpy as np
from jax import lax
from jax.experimental import pallas as pl
from jax.experimental.pallas import tpu as pltpu
from jax.sharding import PartitionSpec as P

band_alpha = 0.4995
MESH = pl.DeviceIdType.MESH


def line_operators(length_all):
    lower_band = np.full(length_all, band_alpha)
    lower_band[[1, length_all - 2]] = 0.25
    lower_band[[0, length_all - 1]] = 0.0
    band = np.eye(length_all)
    rows = np.arange(length_all)
    band[rows[1:], rows[:-1]] = lower_band[1:]
    band[rows[:-1], rows[1:]] = lower_band[:-1]
    near_coef = (band_alpha + 2.0) / 3.0
    far_coef = (4.0 * band_alpha - 1.0) / 12.0
    weights = np.zeros((5, length_all))
    weights[:, :] = np.array([-far_coef, -near_coef, 0.0, near_coef, far_coef])[:, None]
    weights[:, 1] = [0.0, -0.75, 0.0, 0.75, 0.0]
    weights[:, length_all - 2] = [0.0, -0.75, 0.0, 0.75, 0.0]
    weights[:, 0] = [0.0, 0.0, -1.5, 2.0, -0.5]
    weights[:, length_all - 1] = [0.5, -2.0, 1.5, 0.0, 0.0]
    right = np.zeros((length_all, length_all))
    for offset in range(-2, 3):
        good = rows[(rows + offset >= 0) & (rows + offset < length_all)]
        right[good, good + offset] = weights[offset + 2, good]
    inverse = np.linalg.inv(band)
    return inverse, inverse @ right


def block_tables(pieces, block):
    inverse, whole = line_operators(pieces * block)
    own = np.zeros((pieces, block, block))
    fix = np.zeros((pieces, block, 8))
    sends = np.zeros((pieces, 8, block))
    gains = np.zeros((2, pieces, max(pieces - 1, 1)))
    half = block // 2
    for p in range(pieces):
        lo, hi = p * block, (p + 1) * block
        own[p] = whole[lo:hi, lo:hi]
        sends[p, 1, block - 2] = sends[p, 2, block - 1] = 1.0
        sends[p, 4, 0] = sends[p, 5, 1] = 1.0
        if p + 1 < pieces:
            shape = inverse[hi : hi + block, hi - 1] / inverse[hi, hi - 1]
            sends[p, 0] = whole[hi + half, lo:hi] / shape[half]
            fix[p + 1, :, 0] = shape
            near = whole[hi : hi + block, hi - 2 : hi]
            fix[p + 1, :, 1:3] = near - shape[:, None] * sends[p, 0, block - 2 :]
            for d in range(1, pieces - p):
                gains[0, p + d, d - 1] = inverse[lo + d * block, hi - 1] / inverse[hi, hi - 1]
        if p > 0:
            shape = inverse[lo - block : lo, lo] / inverse[lo - 1, lo]
            sends[p, 3] = whole[lo - block + half, lo:hi] / shape[half]
            fix[p - 1, :, 3] = shape
            near = whole[lo - block : lo, lo : lo + 2]
            fix[p - 1, :, 4:6] = near - shape[:, None] * sends[p, 3, :2]
            for d in range(1, p + 1):
                gains[1, p - d, d - 1] = inverse[hi - 1 - d * block, lo] / inverse[lo - 1, lo]
    return own, fix, sends, gains


def split(table):
    high = table.astype(ml_dtypes.bfloat16)
    low = (table - high.astype(np.float64)).astype(ml_dtypes.bfloat16)
    return high, low


def roomy(table):
    pieces, rows, width = table.shape
    more = max(0, (1 << 21) // (pieces * max(width, 256)) - rows)
    return jnp.asarray(np.pad(table, ((0, 0), (0, -(-more // 16) * 16), (0, 0))))


def halves(values):
    high = values.astype(jnp.bfloat16)
    low = (values - high.astype(jnp.float32)).astype(jnp.bfloat16)
    return high, low


def exchange_kernel(
    wall_n, span_n, wall_gains, span_gains,
    f_hbm, wall_tab, span_tab,
    wall_loc, span_loc, wall_msg, span_msg, wall_fix, span_fix,
    f_buf, wall_t, span_t, wall_out, span_out, wall_near, span_near, wall_far, span_far,
    load_sems, table_sems, send_sems, recv_sems,
):
    me_w, me_s, me_c = (lax.axis_index(name) for name in ("wall", "span", "stream"))
    fields, planes, rows, columns = f_hbm.shape
    slabs = fields * planes
    loads = [
        pltpu.make_async_copy(f_hbm.at[k], f_buf.at[pl.ds(k * planes, planes)], load_sems.at[k])
        for k in range(fields)
    ]
    tables = [
        pltpu.make_async_copy(src, dst, table_sems.at[k])
        for k, (src, dst) in enumerate((
            (wall_tab.at[me_w, pl.ds(0, wall_t.shape[0])], wall_t),
            (span_tab.at[me_s, pl.ds(0, span_t.shape[0])], span_t),
        ))
    ]
    for copy in tables[:1] + loads[:2] + tables[1:] + loads[2:]:
        copy.start()

    def device(axis, shift):
        if axis == 0:
            return (me_w + shift, me_s, me_c)
        return (me_w, me_s + shift, me_c)

    axes = ((0, me_w, wall_n), (1, me_s, span_n))
    barrier = pltpu.get_barrier_semaphore()
    for axis, me, n in axes:
        for d in range(1, n):
            @pl.when(me + d < n)
            def _():
                pl.semaphore_signal(barrier, inc=1, device_id=device(axis, d), device_id_type=MESH)

            @pl.when(me >= d)
            def _():
                pl.semaphore_signal(barrier, inc=1, device_id=device(axis, -d), device_id_type=MESH)

    wall_msg[...] = jnp.zeros_like(wall_msg)
    span_msg[...] = jnp.zeros_like(span_msg)
    outs, nears, fars = (wall_out, span_out), (wall_near, span_near), (wall_far, span_far)
    gains = (wall_gains, span_gains)

    def transfer(axis, side, d):
        if d == 1:
            src, dst = outs[axis].at[pl.ds(3 * side, 3)], nears[axis].at[side]
        else:
            src, dst = outs[axis].at[3 * side], fars[axis].at[side, d - 2]
        return pltpu.make_async_remote_copy(
            src_ref=src, dst_ref=dst,
            send_sem=send_sems.at[axis, side, d - 1], recv_sem=recv_sems.at[axis, side, d - 1],
            device_id=device(axis, d if side == 0 else -d), device_id_type=MESH,
        )

    def has_target(me, n, side, d):
        return me + d < n if side == 0 else me >= d

    def has_source(me, n, side, d):
        return me >= d if side == 0 else me + d < n

    def send_all(axis, me, n):
        for d in range(n - 1, 0, -1):
            for side in range(2):
                @pl.when(has_target(me, n, side, d))
                def _():
                    transfer(axis, side, d).start()

    tables[0].wait()
    columns_at = 2 * rows + 16
    picks = wall_t[:rows, columns_at : columns_at + 4].astype(jnp.float32)
    picks = picks[:, :2] + picks[:, 2:]
    wall_a = jnp.broadcast_to(picks[:, 0:1], (rows, columns))
    wall_b = jnp.broadcast_to(picks[:, 1:2], (rows, columns))
    for k in range(fields):
        loads[k].wait()
        here = pl.ds(k * planes, planes)
        values = f_buf[here]
        wall_out[0, here, :] = jnp.sum(values * wall_a[None], axis=1)
        wall_out[3, here, :] = jnp.sum(values * wall_b[None], axis=1)
        wall_out[1, here, :] = f_buf[here, rows - 2, :]
        wall_out[2, here, :] = f_buf[here, rows - 1, :]
        wall_out[4, here, :] = f_buf[here, 0, :]
        wall_out[5, here, :] = f_buf[here, 1, :]
    pl.semaphore_wait(barrier, wall_n + span_n - 2)
    send_all(*axes[0])

    tables[1].wait()
    tiles = planes * rows // 128
    depth = 2 * columns
    for k in range(fields):
        high, low = halves(f_buf[pl.ds(k * planes, planes)].reshape(planes * rows, columns))
        both = jnp.concatenate([high, low], axis=1)
        picked = lax.dot_general(
            span_t[depth : depth + 16], both, (((1,), (1,)), ((), ())), preferred_element_type=jnp.float32
        )
        picked = picked[:8] + picked[8:]
        for t in range(tiles):
            for m in range(6):
                span_out[m, k * tiles + t : k * tiles + t + 1, :] = picked[m : m + 1, t * 128 : (t + 1) * 128]
    send_all(*axes[1])

    wall_fix[...] = wall_t[:, 2 * rows : 2 * rows + 16]
    span_fix[...] = span_t[depth + 16 : depth + 32]
    group = 4

    @pl.loop(0, fields)
    def _(field):
        for part in range(planes // group):
            first = field * planes + part * group
            here = pl.ds(first, group)
            high, low = halves(f_buf[here])
            both = jnp.concatenate([high, low], axis=2).reshape(group * rows, depth)
            spread = jnp.dot(both, span_t[:depth], preferred_element_type=jnp.float32)
            spread = spread[:, :columns] + spread[:, columns:]
            span_loc[here] = spread.reshape(group, rows, columns)
            for q in range(0, group, 2):
                pair = jnp.concatenate(
                    [jnp.concatenate([high[j], low[j]], axis=0) for j in (q, q + 1)], axis=1
                )
                solved = jnp.dot(wall_t[:, : 2 * rows], pair, preferred_element_type=jnp.float32)
                solved = solved[:rows] + solved[rows:]
                wall_loc[first + q] = solved[:, :columns]
                wall_loc[first + q + 1] = solved[:, columns:]

    msgs = (wall_msg, span_msg)
    for axis, me, n in axes:
        for d in range(1, n):
            for side in range(2):
                @pl.when(has_source(me, n, side, d))
                def _():
                    transfer(axis, side, d).wait_recv()
                    gain = jnp.float32(0.0)
                    for p in range(n):
                        gain = jnp.where(me == p, jnp.float32(gains[axis][side, p, d - 1]), gain)
                    if d == 1:
                        msgs[axis][3 * side] += gain * nears[axis][side, 0]
                        msgs[axis][3 * side + 1] = nears[axis][side, 1]
                        msgs[axis][3 * side + 2] = nears[axis][side, 2]
                    else:
                        msgs[axis][3 * side] += gain * fars[axis][side, d - 2]
    for axis, me, n in axes:
        for d in range(1, n):
            for side in range(2):
                @pl.when(has_target(me, n, side, d))
                def _():
                    transfer(axis, side, d).wait_send()


def correct_kernel(
    group, wall_loc, span_loc, wall_metric, span_metric, wall_msg, span_msg, wall_fix, span_fix,
    wall_hbm, span_hbm, wall_buf, span_buf, sems,
):
    planes = wall_metric.shape[0]
    slabs, rows, columns = wall_loc.shape
    tiles = group * rows // 128
    fields = slabs // planes

    def copies(field):
        here = pl.ds(field * planes, planes)
        return (
            pltpu.make_async_copy(wall_buf.at[here], wall_hbm.at[here], sems.at[0, field]),
            pltpu.make_async_copy(span_buf.at[here], span_hbm.at[here], sems.at[1, field]),
        )

    @pl.loop(0, fields)
    def _(field):
        for part in range(planes // group):
            plane = part * group
            first = field * planes + plane
            here = pl.ds(first, group)
            tile = (field * (planes // group) + part) * tiles
            edge = jnp.concatenate([span_msg[:, tile + t, :] for t in range(tiles)], axis=1)
            edge_high, edge_low = halves(edge)
            edges = jnp.concatenate([edge_high.astype(jnp.float32), edge_low.astype(jnp.float32)], axis=0).T
            spread = jnp.dot(edges.astype(jnp.bfloat16), span_fix[...], preferred_element_type=jnp.float32)
            spread = (spread[:, :columns] + spread[:, columns:]).reshape(group, rows, columns)
            span_buf[here] = (span_loc[here] + spread) * span_metric[pl.ds(plane, group)]
            for q in range(0, group, 2):
                msgs = [jnp.concatenate(halves(wall_msg[:, first + j, :]), axis=0) for j in (q, q + 1)]
                solved = jnp.dot(wall_fix[...], jnp.concatenate(msgs, axis=1), preferred_element_type=jnp.float32)
                solved = solved[:rows] + solved[rows:]
                for j in range(2):
                    wall_buf[first + q + j] = (
                        wall_loc[first + q + j] + solved[:, j * columns : (j + 1) * columns]
                    ) * wall_metric[plane + q + j]
        for copy in copies(field):
            copy.start()

    @pl.loop(0, fields)
    def _(field):
        for copy in copies(field):
            copy.wait()


def per_device(wall_n, span_n, conserved, wall_metric, span_metric):
    fields, planes, rows, columns = conserved.shape
    slabs = fields * planes
    lines = slabs * rows // 128
    own_w, fix_w, sends_w, gains_w = block_tables(wall_n, rows)
    own_s, fix_s, sends_s, gains_s = block_tables(span_n, columns)
    f32, bf16 = jnp.float32, jnp.bfloat16

    own_high, own_low = split(own_w)
    fix_high, fix_low = split(fix_w)
    picks = np.concatenate(split(sends_w[:, (0, 3)].transpose(0, 2, 1)), axis=2)
    wall_tab = np.concatenate([
        np.concatenate([own_high, own_high, fix_high, fix_high, picks], axis=2),
        np.concatenate([own_low, own_low, fix_low, fix_low, picks], axis=2),
    ], axis=1)
    own_high, own_low = split(own_s.transpose(0, 2, 1))
    sends_high, sends_low = split(sends_s)
    fix_high, fix_low = split(fix_s.transpose(0, 2, 1))
    span_tab = np.concatenate(
        [np.concatenate([own_high, own_low], axis=2)] * 2
        + [np.concatenate([t, t], axis=2) for t in (sends_high, sends_low)]
        + [np.concatenate([fix_high, fix_low], axis=2)] * 2,
        axis=1,
    )

    vmem = pl.BlockSpec(memory_space=pltpu.VMEM)
    hbm = pl.BlockSpec(memory_space=pltpu.HBM)
    far = max(wall_n, span_n) - 1
    flat = (slabs, rows, columns)
    local = pl.pallas_call(
        functools.partial(exchange_kernel, wall_n, span_n, gains_w, gains_s),
        out_shape=(
            jax.ShapeDtypeStruct(flat, f32),
            jax.ShapeDtypeStruct(flat, f32),
            jax.ShapeDtypeStruct((8, slabs, 128), f32),
            jax.ShapeDtypeStruct((8, lines, 128), f32),
            jax.ShapeDtypeStruct((2 * rows, 16), bf16),
            jax.ShapeDtypeStruct((16, 2 * columns), bf16),
        ),
        in_specs=[hbm] * 3,
        out_specs=(vmem,) * 6,
        scratch_shapes=[
            pltpu.VMEM(flat, f32),
            pltpu.VMEM(wall_tab.shape[1:], bf16),
            pltpu.VMEM(span_tab.shape[1:], bf16),
            pltpu.VMEM((6, slabs, 128), f32),
            pltpu.VMEM((6, lines, 128), f32),
            pltpu.VMEM((2, 3, slabs, 128), f32),
            pltpu.VMEM((2, 3, lines, 128), f32),
            pltpu.VMEM((2, max(wall_n - 2, 1), slabs, 128), f32),
            pltpu.VMEM((2, max(span_n - 2, 1), lines, 128), f32),
            pltpu.SemaphoreType.DMA((fields,)),
            pltpu.SemaphoreType.DMA((2,)),
            pltpu.SemaphoreType.DMA((2, 2, far)),
            pltpu.SemaphoreType.DMA((2, 2, far)),
        ],
        compiler_params=pltpu.CompilerParams(
            collective_id=0, has_side_effects=True, vmem_limit_bytes=43 * 1024 * 1024
        ),
        name="exchange",
    )(conserved, roomy(wall_tab), roomy(span_tab))

    group = 4
    outs = pl.pallas_call(
        functools.partial(correct_kernel, group),
        out_shape=(jax.ShapeDtypeStruct(flat, f32),) * 2,
        in_specs=[vmem] * 8,
        out_specs=(hbm, hbm),
        scratch_shapes=[
            pltpu.VMEM(flat, f32), pltpu.VMEM(flat, f32), pltpu.SemaphoreType.DMA((2, fields)),
        ],
        compiler_params=pltpu.CompilerParams(vmem_limit_bytes=24 * 1024 * 1024),
        cost_estimate=pl.CostEstimate(
            flops=2 * slabs * rows * columns * 16 * 8, bytes_accessed=8 * conserved.size, transcendentals=0
        ),
        name="correct",
    )(local[0], local[1], wall_metric, span_metric, *local[2:])
    return tuple(out.reshape(conserved.shape) for out in outs)


def solution(mesh):
    in_specs = (
        P(None, "stream", "wall", "span"),
        P("stream", "wall", "span"),
        P("stream", "wall", "span"),
    )
    out_specs = (P(None, "stream", "wall", "span"), P(None, "stream", "wall", "span"))
    sizes = (mesh.shape["wall"], mesh.shape["span"])
    return jax.shard_map(
        functools.partial(per_device, *sizes), mesh=mesh, in_specs=in_specs, out_specs=out_specs, check_vma=False
    )
```

```python
import functools

import jax
import jax.numpy as jnp
import ml_dtypes
import numpy as np
from jax import lax
from jax.experimental import pallas as pl
from jax.experimental.pallas import tpu as pltpu
from jax.sharding import PartitionSpec as P

band_alpha = 0.4995
MESH = pl.DeviceIdType.MESH


def line_operators(length_all):
    lower_band = np.full(length_all, band_alpha)
    lower_band[[1, length_all - 2]] = 0.25
    lower_band[[0, length_all - 1]] = 0.0
    band = np.eye(length_all)
    rows = np.arange(length_all)
    band[rows[1:], rows[:-1]] = lower_band[1:]
    band[rows[:-1], rows[1:]] = lower_band[:-1]
    near_coef = (band_alpha + 2.0) / 3.0
    far_coef = (4.0 * band_alpha - 1.0) / 12.0
    weights = np.zeros((5, length_all))
    weights[:, :] = np.array([-far_coef, -near_coef, 0.0, near_coef, far_coef])[:, None]
    weights[:, 1] = [0.0, -0.75, 0.0, 0.75, 0.0]
    weights[:, length_all - 2] = [0.0, -0.75, 0.0, 0.75, 0.0]
    weights[:, 0] = [0.0, 0.0, -1.5, 2.0, -0.5]
    weights[:, length_all - 1] = [0.5, -2.0, 1.5, 0.0, 0.0]
    right = np.zeros((length_all, length_all))
    for offset in range(-2, 3):
        good = rows[(rows + offset >= 0) & (rows + offset < length_all)]
        right[good, good + offset] = weights[offset + 2, good]
    inverse = np.linalg.inv(band)
    return inverse, inverse @ right


def block_tables(pieces, block):
    inverse, whole = line_operators(pieces * block)
    own = np.zeros((pieces, block, block))
    fix = np.zeros((pieces, block, 8))
    sends = np.zeros((pieces, 8, block))
    gains = np.zeros((2, pieces, max(pieces - 1, 1)))
    half = block // 2
    for p in range(pieces):
        lo, hi = p * block, (p + 1) * block
        own[p] = whole[lo:hi, lo:hi]
        sends[p, 1, block - 2] = sends[p, 2, block - 1] = 1.0
        sends[p, 4, 0] = sends[p, 5, 1] = 1.0
        if p + 1 < pieces:
            shape = inverse[hi : hi + block, hi - 1] / inverse[hi, hi - 1]
            sends[p, 0] = whole[hi + half, lo:hi] / shape[half]
            fix[p + 1, :, 0] = shape
            near = whole[hi : hi + block, hi - 2 : hi]
            fix[p + 1, :, 1:3] = near - shape[:, None] * sends[p, 0, block - 2 :]
            for d in range(1, pieces - p):
                gains[0, p + d, d - 1] = inverse[lo + d * block, hi - 1] / inverse[hi, hi - 1]
        if p > 0:
            shape = inverse[lo - block : lo, lo] / inverse[lo - 1, lo]
            sends[p, 3] = whole[lo - block + half, lo:hi] / shape[half]
            fix[p - 1, :, 3] = shape
            near = whole[lo - block : lo, lo : lo + 2]
            fix[p - 1, :, 4:6] = near - shape[:, None] * sends[p, 3, :2]
            for d in range(1, p + 1):
                gains[1, p - d, d - 1] = inverse[hi - 1 - d * block, lo] / inverse[lo - 1, lo]
    return own, fix, sends, gains


def split(table):
    high = table.astype(ml_dtypes.bfloat16)
    low = (table - high.astype(np.float64)).astype(ml_dtypes.bfloat16)
    return high, low


def roomy(table):
    pieces, rows, width = table.shape
    more = max(0, (1 << 21) // (pieces * max(width, 256)) - rows)
    return jnp.asarray(np.pad(table, ((0, 0), (0, -(-more // 16) * 16), (0, 0))))


def halves(values):
    high = values.astype(jnp.bfloat16)
    low = (values - high.astype(jnp.float32)).astype(jnp.bfloat16)
    return high, low


def exchange_kernel(
    wall_n, span_n, wall_gains, span_gains,
    f_hbm, wall_tab, span_tab,
    wall_loc, span_loc, wall_msg, span_msg, wall_fix, span_fix,
    f_buf, wall_t, span_t, wall_out, span_out, wall_near, span_near, wall_far, span_far,
    load_sems, table_sems, send_sems, recv_sems,
):
    me_w, me_s, me_c = (lax.axis_index(name) for name in ("wall", "span", "stream"))
    fields, planes, rows, columns = f_hbm.shape
    slabs = fields * planes
    loads = [
        pltpu.make_async_copy(f_hbm.at[k], f_buf.at[pl.ds(k * planes, planes)], load_sems.at[k])
        for k in range(fields)
    ]
    tables = [
        pltpu.make_async_copy(src, dst, table_sems.at[k])
        for k, (src, dst) in enumerate((
            (wall_tab.at[me_w, pl.ds(0, wall_t.shape[0])], wall_t),
            (span_tab.at[me_s, pl.ds(0, span_t.shape[0])], span_t),
        ))
    ]
    for copy in tables[:1] + loads[:2] + tables[1:] + loads[2:]:
        copy.start()

    def device(axis, shift):
        if axis == 0:
            return (me_w + shift, me_s, me_c)
        return (me_w, me_s + shift, me_c)

    axes = ((0, me_w, wall_n), (1, me_s, span_n))
    barrier = pltpu.get_barrier_semaphore()
    for axis, me, n in axes:
        for d in range(1, n):
            @pl.when(me + d < n)
            def _():
                pl.semaphore_signal(barrier, inc=1, device_id=device(axis, d), device_id_type=MESH)

            @pl.when(me >= d)
            def _():
                pl.semaphore_signal(barrier, inc=1, device_id=device(axis, -d), device_id_type=MESH)

    wall_msg[...] = jnp.zeros_like(wall_msg)
    span_msg[...] = jnp.zeros_like(span_msg)
    outs, nears, fars = (wall_out, span_out), (wall_near, span_near), (wall_far, span_far)
    gains = (wall_gains, span_gains)

    def transfer(axis, side, d):
        if d == 1:
            src, dst = outs[axis].at[pl.ds(3 * side, 3)], nears[axis].at[side]
        else:
            src, dst = outs[axis].at[3 * side], fars[axis].at[side, d - 2]
        return pltpu.make_async_remote_copy(
            src_ref=src, dst_ref=dst,
            send_sem=send_sems.at[axis, side, d - 1], recv_sem=recv_sems.at[axis, side, d - 1],
            device_id=device(axis, d if side == 0 else -d), device_id_type=MESH,
        )

    def has_target(me, n, side, d):
        return me + d < n if side == 0 else me >= d

    def has_source(me, n, side, d):
        return me >= d if side == 0 else me + d < n

    def send_all(axis, me, n):
        for d in range(n - 1, 0, -1):
            for side in range(2):
                @pl.when(has_target(me, n, side, d))
                def _():
                    transfer(axis, side, d).start()

    tables[0].wait()
    columns_at = 2 * rows + 32
    picks = wall_t[:rows, columns_at : columns_at + 4].astype(jnp.float32)
    picks = picks[:, :2] + picks[:, 2:]
    wall_a = jnp.broadcast_to(picks[:, 0:1], (rows, columns))
    wall_b = jnp.broadcast_to(picks[:, 1:2], (rows, columns))
    for k in range(fields):
        loads[k].wait()
        here = pl.ds(k * planes, planes)
        values = f_buf[here]
        wall_out[0, here, :] = jnp.sum(values * wall_a[None], axis=1)
        wall_out[3, here, :] = jnp.sum(values * wall_b[None], axis=1)
        wall_out[1, here, :] = f_buf[here, rows - 2, :]
        wall_out[2, here, :] = f_buf[here, rows - 1, :]
        wall_out[4, here, :] = f_buf[here, 0, :]
        wall_out[5, here, :] = f_buf[here, 1, :]
    tables[1].wait()
    tiles = planes * rows // 128
    depth = 2 * columns
    group = 4

    def span_functionals():
        for k in range(fields):
            high, low = halves(f_buf[pl.ds(k * planes, planes)].reshape(planes * rows, columns))
            both = jnp.concatenate([high, low], axis=1)
            picked = lax.dot_general(
                span_t[depth : depth + 16], both, (((1,), (1,)), ((), ())), preferred_element_type=jnp.float32
            )
            picked = picked[:8] + picked[8:]
            for t in range(tiles):
                for m in range(6):
                    span_out[m, k * tiles + t : k * tiles + t + 1, :] = picked[m : m + 1, t * 128 : (t + 1) * 128]

    def local_products():
        @pl.loop(0, fields)
        def _(field):
            for part in range(planes // group):
                first = field * planes + part * group
                here = pl.ds(first, group)
                high, low = halves(f_buf[here])
                both = jnp.concatenate([high, low], axis=2).reshape(group * rows, depth)
                spread = jnp.dot(both, span_t[:depth], preferred_element_type=jnp.float32)
                spread = spread[:, :columns] + spread[:, columns:]
                span_loc[here] = spread.reshape(group, rows, columns)
                for q in range(0, group, 2):
                    pair = jnp.concatenate(
                        [jnp.concatenate([high[j], low[j]], axis=0) for j in (q, q + 1)], axis=1
                    )
                    solved = jnp.dot(wall_t[:, : 2 * rows], pair, preferred_element_type=jnp.float32)
                    solved = solved[:rows] + solved[rows:]
                    wall_loc[first + q] = solved[:, :columns]
                    wall_loc[first + q + 1] = solved[:, columns:]

    early = 2 * me_w < wall_n

    @pl.when(early)
    def _():
        span_functionals()
        local_products()

    pl.semaphore_wait(barrier, wall_n + span_n - 2)
    send_all(*axes[0])

    @pl.when(jnp.logical_not(early))
    def _():
        span_functionals()

    send_all(*axes[1])

    @pl.when(jnp.logical_not(early))
    def _():
        local_products()

    wall_fix[...] = wall_t[:rows, 2 * rows : 2 * rows + 32]
    span_fix[...] = span_t[depth + 16 : depth + 48, :columns]

    msgs = (wall_msg, span_msg)
    for axis, me, n in axes:
        for d in range(1, n):
            for side in range(2):
                @pl.when(has_source(me, n, side, d))
                def _():
                    transfer(axis, side, d).wait_recv()
                    gain = jnp.float32(0.0)
                    for p in range(n):
                        gain = jnp.where(me == p, jnp.float32(gains[axis][side, p, d - 1]), gain)
                    if d == 1:
                        msgs[axis][3 * side] += gain * nears[axis][side, 0]
                        msgs[axis][3 * side + 1] = nears[axis][side, 1]
                        msgs[axis][3 * side + 2] = nears[axis][side, 2]
                    else:
                        msgs[axis][3 * side] += gain * fars[axis][side, d - 2]
    for axis, me, n in axes:
        for d in range(1, n):
            for side in range(2):
                @pl.when(has_target(me, n, side, d))
                def _():
                    transfer(axis, side, d).wait_send()


def correct_kernel(
    group, wall_loc, span_loc, wall_metric, span_metric, wall_msg, span_msg, wall_fix, span_fix,
    wall_hbm, span_hbm, wall_buf, span_buf, sems,
):
    planes = wall_metric.shape[0]
    slabs, rows, columns = wall_loc.shape
    tiles = group * rows // 128
    fields = slabs // planes

    def copies(field):
        here = pl.ds(field * planes, planes)
        return (
            pltpu.make_async_copy(wall_buf.at[here], wall_hbm.at[here], sems.at[0, field]),
            pltpu.make_async_copy(span_buf.at[here], span_hbm.at[here], sems.at[1, field]),
        )

    @pl.loop(0, fields)
    def _(field):
        for part in range(planes // group):
            plane = part * group
            first = field * planes + plane
            here = pl.ds(first, group)
            tile = (field * (planes // group) + part) * tiles
            edge = jnp.concatenate([span_msg[:, tile + t, :] for t in range(tiles)], axis=1)
            edge_high, edge_low = halves(edge)
            edges = [edge_high.astype(jnp.float32), edge_low.astype(jnp.float32)] * 2
            edges = jnp.concatenate(edges, axis=0).T.astype(jnp.bfloat16)
            spread = jnp.dot(edges, span_fix[...], preferred_element_type=jnp.float32)
            spread = spread.reshape(group, rows, columns)
            span_buf[here] = (span_loc[here] + spread) * span_metric[pl.ds(plane, group)]
            for q in range(0, group, 2):
                msgs = [jnp.concatenate(halves(wall_msg[:, first + j, :]) * 2, axis=0) for j in (q, q + 1)]
                solved = jnp.dot(wall_fix[...], jnp.concatenate(msgs, axis=1), preferred_element_type=jnp.float32)
                for j in range(2):
                    wall_buf[first + q + j] = (
                        wall_loc[first + q + j] + solved[:, j * columns : (j + 1) * columns]
                    ) * wall_metric[plane + q + j]
        for copy in copies(field):
            copy.start()

    @pl.loop(0, fields)
    def _(field):
        for copy in copies(field):
            copy.wait()


def per_device(wall_n, span_n, conserved, wall_metric, span_metric):
    fields, planes, rows, columns = conserved.shape
    slabs = fields * planes
    lines = slabs * rows // 128
    own_w, fix_w, sends_w, gains_w = block_tables(wall_n, rows)
    own_s, fix_s, sends_s, gains_s = block_tables(span_n, columns)
    f32, bf16 = jnp.float32, jnp.bfloat16

    own_high, own_low = split(own_w)
    fix_high, fix_low = split(fix_w)
    picks = np.concatenate(split(sends_w[:, (0, 3)].transpose(0, 2, 1)), axis=2)
    wall_tab = np.concatenate([
        np.concatenate([own_high, own_high, fix_high, fix_high, fix_low, fix_low, picks], axis=2),
        np.concatenate([own_low, own_low, fix_high, fix_high, fix_low, fix_low, picks], axis=2),
    ], axis=1)
    own_high, own_low = split(own_s.transpose(0, 2, 1))
    sends_high, sends_low = split(sends_s)
    fix_high, fix_low = split(fix_s.transpose(0, 2, 1))
    span_tab = np.concatenate(
        [np.concatenate([own_high, own_low], axis=2)] * 2
        + [np.concatenate([t, t], axis=2) for t in (sends_high, sends_low)]
        + [np.concatenate([t, t], axis=2) for t in (fix_high, fix_high, fix_low, fix_low)],
        axis=1,
    )

    vmem = pl.BlockSpec(memory_space=pltpu.VMEM)
    hbm = pl.BlockSpec(memory_space=pltpu.HBM)
    far = max(wall_n, span_n) - 1
    flat = (slabs, rows, columns)
    local = pl.pallas_call(
        functools.partial(exchange_kernel, wall_n, span_n, gains_w, gains_s),
        out_shape=(
            jax.ShapeDtypeStruct(flat, f32),
            jax.ShapeDtypeStruct(flat, f32),
            jax.ShapeDtypeStruct((8, slabs, 128), f32),
            jax.ShapeDtypeStruct((8, lines, 128), f32),
            jax.ShapeDtypeStruct((rows, 32), bf16),
            jax.ShapeDtypeStruct((32, columns), bf16),
        ),
        in_specs=[hbm] * 3,
        out_specs=(vmem,) * 6,
        scratch_shapes=[
            pltpu.VMEM(flat, f32),
            pltpu.VMEM(wall_tab.shape[1:], bf16),
            pltpu.VMEM(span_tab.shape[1:], bf16),
            pltpu.VMEM((6, slabs, 128), f32),
            pltpu.VMEM((6, lines, 128), f32),
            pltpu.VMEM((2, 3, slabs, 128), f32),
            pltpu.VMEM((2, 3, lines, 128), f32),
            pltpu.VMEM((2, max(wall_n - 2, 1), slabs, 128), f32),
            pltpu.VMEM((2, max(span_n - 2, 1), lines, 128), f32),
            pltpu.SemaphoreType.DMA((fields,)),
            pltpu.SemaphoreType.DMA((2,)),
            pltpu.SemaphoreType.DMA((2, 2, far)),
            pltpu.SemaphoreType.DMA((2, 2, far)),
        ],
        compiler_params=pltpu.CompilerParams(
            collective_id=0, has_side_effects=True, vmem_limit_bytes=43 * 1024 * 1024
        ),
        name="exchange",
    )(conserved, roomy(wall_tab), roomy(span_tab))

    group = 4
    outs = pl.pallas_call(
        functools.partial(correct_kernel, group),
        out_shape=(jax.ShapeDtypeStruct(flat, f32),) * 2,
        in_specs=[vmem] * 8,
        out_specs=(hbm, hbm),
        scratch_shapes=[
            pltpu.VMEM(flat, f32), pltpu.VMEM(flat, f32), pltpu.SemaphoreType.DMA((2, fields)),
        ],
        compiler_params=pltpu.CompilerParams(vmem_limit_bytes=24 * 1024 * 1024),
        cost_estimate=pl.CostEstimate(
            flops=2 * slabs * rows * columns * 16 * 8, bytes_accessed=8 * conserved.size, transcendentals=0
        ),
        name="correct",
    )(local[0], local[1], wall_metric, span_metric, *local[2:])
    return tuple(out.reshape(conserved.shape) for out in outs)


def solution(mesh):
    in_specs = (
        P(None, "stream", "wall", "span"),
        P("stream", "wall", "span"),
        P("stream", "wall", "span"),
    )
    out_specs = (P(None, "stream", "wall", "span"), P(None, "stream", "wall", "span"))
    sizes = (mesh.shape["wall"], mesh.shape["span"])
    return jax.shard_map(
        functools.partial(per_device, *sizes), mesh=mesh, in_specs=in_specs, out_specs=out_specs, check_vma=False
    )
```

```python
import functools

import jax
import jax.numpy as jnp
import ml_dtypes
import numpy as np
from jax import lax
from jax.experimental import pallas as pl
from jax.experimental.pallas import tpu as pltpu
from jax.sharding import PartitionSpec as P

band_alpha = 0.4995
MESH = pl.DeviceIdType.MESH


def line_operators(length_all):
    lower_band = np.full(length_all, band_alpha)
    lower_band[[1, length_all - 2]] = 0.25
    lower_band[[0, length_all - 1]] = 0.0
    band = np.eye(length_all)
    rows = np.arange(length_all)
    band[rows[1:], rows[:-1]] = lower_band[1:]
    band[rows[:-1], rows[1:]] = lower_band[:-1]
    near_coef = (band_alpha + 2.0) / 3.0
    far_coef = (4.0 * band_alpha - 1.0) / 12.0
    weights = np.zeros((5, length_all))
    weights[:, :] = np.array([-far_coef, -near_coef, 0.0, near_coef, far_coef])[:, None]
    weights[:, 1] = [0.0, -0.75, 0.0, 0.75, 0.0]
    weights[:, length_all - 2] = [0.0, -0.75, 0.0, 0.75, 0.0]
    weights[:, 0] = [0.0, 0.0, -1.5, 2.0, -0.5]
    weights[:, length_all - 1] = [0.5, -2.0, 1.5, 0.0, 0.0]
    right = np.zeros((length_all, length_all))
    for offset in range(-2, 3):
        good = rows[(rows + offset >= 0) & (rows + offset < length_all)]
        right[good, good + offset] = weights[offset + 2, good]
    inverse = np.linalg.inv(band)
    return inverse, inverse @ right


def block_tables(pieces, block):
    inverse, whole = line_operators(pieces * block)
    own = np.zeros((pieces, block, block))
    fix = np.zeros((pieces, block, 8))
    sends = np.zeros((pieces, 8, block))
    gains = np.zeros((2, pieces, max(pieces - 1, 1)))
    half = block // 2
    for p in range(pieces):
        lo, hi = p * block, (p + 1) * block
        own[p] = whole[lo:hi, lo:hi]
        sends[p, 1, block - 2] = sends[p, 2, block - 1] = 1.0
        sends[p, 4, 0] = sends[p, 5, 1] = 1.0
        if p + 1 < pieces:
            shape = inverse[hi : hi + block, hi - 1] / inverse[hi, hi - 1]
            sends[p, 0] = whole[hi + half, lo:hi] / shape[half]
            fix[p + 1, :, 0] = shape
            near = whole[hi : hi + block, hi - 2 : hi]
            fix[p + 1, :, 1:3] = near - shape[:, None] * sends[p, 0, block - 2 :]
            for d in range(1, pieces - p):
                gains[0, p + d, d - 1] = inverse[lo + d * block, hi - 1] / inverse[hi, hi - 1]
        if p > 0:
            shape = inverse[lo - block : lo, lo] / inverse[lo - 1, lo]
            sends[p, 3] = whole[lo - block + half, lo:hi] / shape[half]
            fix[p - 1, :, 3] = shape
            near = whole[lo - block : lo, lo : lo + 2]
            fix[p - 1, :, 4:6] = near - shape[:, None] * sends[p, 3, :2]
            for d in range(1, p + 1):
                gains[1, p - d, d - 1] = inverse[hi - 1 - d * block, lo] / inverse[lo - 1, lo]
    return own, fix, sends, gains


def split(table):
    high = table.astype(ml_dtypes.bfloat16)
    low = (table - high.astype(np.float64)).astype(ml_dtypes.bfloat16)
    return high, low


def roomy(table):
    pieces, rows, width = table.shape
    more = max(0, (1 << 21) // (pieces * max(width, 256)) - rows)
    return jnp.asarray(np.pad(table, ((0, 0), (0, -(-more // 16) * 16), (0, 0))))


def halves(values):
    high = values.astype(jnp.bfloat16)
    low = (values - high.astype(jnp.float32)).astype(jnp.bfloat16)
    return high, low


def exchange_kernel(
    wall_n, span_n, wall_gains, span_gains,
    f_hbm, wall_tab, span_tab,
    wall_loc, span_loc, wall_msg, span_msg, wall_fix, span_fix,
    f_buf, wall_t, span_t, wall_out, span_out, wall_near, span_near, wall_far, span_far,
    load_sems, table_sems, send_sems, recv_sems,
):
    me_w, me_s, me_c = (lax.axis_index(name) for name in ("wall", "span", "stream"))
    fields, planes, rows, columns = f_hbm.shape
    slabs = fields * planes
    loads = [
        pltpu.make_async_copy(f_hbm.at[k], f_buf.at[pl.ds(k * planes, planes)], load_sems.at[k])
        for k in range(fields)
    ]
    tables = [
        pltpu.make_async_copy(src, dst, table_sems.at[k])
        for k, (src, dst) in enumerate((
            (wall_tab.at[me_w, pl.ds(0, wall_t.shape[0])], wall_t),
            (span_tab.at[me_s, pl.ds(0, span_t.shape[0])], span_t),
        ))
    ]
    for copy in tables[:1] + loads[:2] + tables[1:] + loads[2:]:
        copy.start()

    def device(axis, shift):
        if axis == 0:
            return (me_w + shift, me_s, me_c)
        return (me_w, me_s + shift, me_c)

    axes = ((0, me_w, wall_n), (1, me_s, span_n))
    barrier = pltpu.get_barrier_semaphore()
    for axis, me, n in axes:
        for d in range(1, n):
            @pl.when(me + d < n)
            def _():
                pl.semaphore_signal(barrier, inc=1, device_id=device(axis, d), device_id_type=MESH)

            @pl.when(me >= d)
            def _():
                pl.semaphore_signal(barrier, inc=1, device_id=device(axis, -d), device_id_type=MESH)

    wall_msg[...] = jnp.zeros_like(wall_msg)
    span_msg[...] = jnp.zeros_like(span_msg)
    outs, nears, fars = (wall_out, span_out), (wall_near, span_near), (wall_far, span_far)
    gains = (wall_gains, span_gains)

    def transfer(axis, side, d):
        if d == 1:
            src, dst = outs[axis].at[pl.ds(3 * side, 3)], nears[axis].at[side]
        else:
            src, dst = outs[axis].at[3 * side], fars[axis].at[side, d - 2]
        return pltpu.make_async_remote_copy(
            src_ref=src, dst_ref=dst,
            send_sem=send_sems.at[axis, side, d - 1], recv_sem=recv_sems.at[axis, side, d - 1],
            device_id=device(axis, d if side == 0 else -d), device_id_type=MESH,
        )

    def has_target(me, n, side, d):
        return me + d < n if side == 0 else me >= d

    def has_source(me, n, side, d):
        return me >= d if side == 0 else me + d < n

    def send_all(axis, me, n):
        for d in range(n - 1, 0, -1):
            for side in range(2):
                @pl.when(has_target(me, n, side, d))
                def _():
                    transfer(axis, side, d).start()

    tables[0].wait()
    columns_at = 2 * rows + 32
    picks = wall_t[:rows, columns_at : columns_at + 4].astype(jnp.float32)
    picks = picks[:, :2] + picks[:, 2:]
    wall_a = jnp.broadcast_to(picks[:, 0:1], (rows, columns))
    wall_b = jnp.broadcast_to(picks[:, 1:2], (rows, columns))
    for k in range(fields):
        loads[k].wait()
        here = pl.ds(k * planes, planes)
        sums = [jnp.zeros((planes, 8, columns), jnp.float32)] * 2
        for r in range(0, rows, 8):
            values = f_buf[here, r : r + 8, :]
            sums = [total + values * v[None, r : r + 8] for total, v in zip(sums, (wall_a, wall_b))]
        wall_out[0, here, :] = jnp.sum(sums[0], axis=1)
        wall_out[3, here, :] = jnp.sum(sums[1], axis=1)
        wall_out[1, here, :] = f_buf[here, rows - 2, :]
        wall_out[2, here, :] = f_buf[here, rows - 1, :]
        wall_out[4, here, :] = f_buf[here, 0, :]
        wall_out[5, here, :] = f_buf[here, 1, :]
    tiles = planes * rows // 128
    depth = 2 * columns
    group = 4

    def span_functionals():
        for k in range(fields):
            high, low = halves(f_buf[pl.ds(k * planes, planes)].reshape(planes * rows, columns))
            both = jnp.concatenate([high, low], axis=1)
            picked = lax.dot_general(
                span_t[depth : depth + 16], both, (((1,), (1,)), ((), ())), preferred_element_type=jnp.float32
            )
            picked = picked[:8] + picked[8:]
            for t in range(tiles):
                for m in range(6):
                    span_out[m, k * tiles + t : k * tiles + t + 1, :] = picked[m : m + 1, t * 128 : (t + 1) * 128]

    def local_products():
        @pl.loop(0, fields)
        def _(field):
            for part in range(planes // group):
                first = field * planes + part * group
                here = pl.ds(first, group)
                high, low = halves(f_buf[here])
                both = jnp.concatenate([high, low], axis=2).reshape(group * rows, depth)
                spread = jnp.dot(both, span_t[:depth], preferred_element_type=jnp.float32)
                spread = spread[:, :columns] + spread[:, columns:]
                span_loc[here] = spread.reshape(group, rows, columns)
                for q in range(0, group, 2):
                    pair = jnp.concatenate(
                        [jnp.concatenate([high[j], low[j]], axis=0) for j in (q, q + 1)], axis=1
                    )
                    solved = jnp.dot(wall_t[:, : 2 * rows], pair, preferred_element_type=jnp.float32)
                    solved = solved[:rows] + solved[rows:]
                    wall_loc[first + q] = solved[:, :columns]
                    wall_loc[first + q + 1] = solved[:, columns:]

    pl.semaphore_wait(barrier, wall_n + span_n - 2)
    send_all(*axes[0])
    tables[1].wait()
    span_functionals()
    send_all(*axes[1])
    local_products()

    wall_fix[...] = wall_t[:rows, 2 * rows : 2 * rows + 32]
    span_fix[...] = span_t[depth + 16 : depth + 48, :columns]

    msgs = (wall_msg, span_msg)
    for axis, me, n in axes:
        for d in range(1, n):
            for side in range(2):
                @pl.when(has_source(me, n, side, d))
                def _():
                    transfer(axis, side, d).wait_recv()
                    gain = jnp.float32(0.0)
                    for p in range(n):
                        gain = jnp.where(me == p, jnp.float32(gains[axis][side, p, d - 1]), gain)
                    if d == 1:
                        msgs[axis][3 * side] += gain * nears[axis][side, 0]
                        msgs[axis][3 * side + 1] = nears[axis][side, 1]
                        msgs[axis][3 * side + 2] = nears[axis][side, 2]
                    else:
                        msgs[axis][3 * side] += gain * fars[axis][side, d - 2]
    for axis, me, n in axes:
        for d in range(1, n):
            for side in range(2):
                @pl.when(has_target(me, n, side, d))
                def _():
                    transfer(axis, side, d).wait_send()


def correct_kernel(
    group, wall_loc, span_loc, wall_metric, span_metric, wall_msg, span_msg, wall_fix, span_fix,
    wall_hbm, span_hbm, wall_buf, span_buf, sems,
):
    planes = wall_metric.shape[0]
    slabs, rows, columns = wall_loc.shape
    tiles = group * rows // 128
    fields = slabs // planes

    def copies(field):
        here = pl.ds(field * planes, planes)
        return (
            pltpu.make_async_copy(wall_buf.at[here], wall_hbm.at[here], sems.at[0, field]),
            pltpu.make_async_copy(span_buf.at[here], span_hbm.at[here], sems.at[1, field]),
        )

    @pl.loop(0, fields)
    def _(field):
        for part in range(planes // group):
            plane = part * group
            first = field * planes + plane
            here = pl.ds(first, group)
            tile = (field * (planes // group) + part) * tiles
            edge = jnp.concatenate([span_msg[:, tile + t, :] for t in range(tiles)], axis=1)
            edge_high, edge_low = halves(edge)
            edges = [edge_high.astype(jnp.float32), edge_low.astype(jnp.float32)] * 2
            edges = jnp.concatenate(edges, axis=0).T.astype(jnp.bfloat16)
            spread = jnp.dot(edges, span_fix[...], preferred_element_type=jnp.float32)
            spread = spread.reshape(group, rows, columns)
            span_buf[here] = (span_loc[here] + spread) * span_metric[pl.ds(plane, group)]
            for q in range(0, group, 2):
                msgs = [jnp.concatenate(halves(wall_msg[:, first + j, :]) * 2, axis=0) for j in (q, q + 1)]
                solved = jnp.dot(wall_fix[...], jnp.concatenate(msgs, axis=1), preferred_element_type=jnp.float32)
                for j in range(2):
                    wall_buf[first + q + j] = (
                        wall_loc[first + q + j] + solved[:, j * columns : (j + 1) * columns]
                    ) * wall_metric[plane + q + j]
        for copy in copies(field):
            copy.start()

    @pl.loop(0, fields)
    def _(field):
        for copy in copies(field):
            copy.wait()


def per_device(wall_n, span_n, conserved, wall_metric, span_metric):
    fields, planes, rows, columns = conserved.shape
    slabs = fields * planes
    lines = slabs * rows // 128
    own_w, fix_w, sends_w, gains_w = block_tables(wall_n, rows)
    own_s, fix_s, sends_s, gains_s = block_tables(span_n, columns)
    f32, bf16 = jnp.float32, jnp.bfloat16

    own_high, own_low = split(own_w)
    fix_high, fix_low = split(fix_w)
    picks = np.concatenate(split(sends_w[:, (0, 3)].transpose(0, 2, 1)), axis=2)
    wall_tab = np.concatenate([
        np.concatenate([own_high, own_high, fix_high, fix_high, fix_low, fix_low, picks], axis=2),
        np.concatenate([own_low, own_low, fix_high, fix_high, fix_low, fix_low, picks], axis=2),
    ], axis=1)
    own_high, own_low = split(own_s.transpose(0, 2, 1))
    sends_high, sends_low = split(sends_s)
    fix_high, fix_low = split(fix_s.transpose(0, 2, 1))
    span_tab = np.concatenate(
        [np.concatenate([own_high, own_low], axis=2)] * 2
        + [np.concatenate([t, t], axis=2) for t in (sends_high, sends_low)]
        + [np.concatenate([t, t], axis=2) for t in (fix_high, fix_high, fix_low, fix_low)],
        axis=1,
    )

    vmem = pl.BlockSpec(memory_space=pltpu.VMEM)
    hbm = pl.BlockSpec(memory_space=pltpu.HBM)
    far = max(wall_n, span_n) - 1
    flat = (slabs, rows, columns)
    local = pl.pallas_call(
        functools.partial(exchange_kernel, wall_n, span_n, gains_w, gains_s),
        out_shape=(
            jax.ShapeDtypeStruct(flat, f32),
            jax.ShapeDtypeStruct(flat, f32),
            jax.ShapeDtypeStruct((8, slabs, 128), f32),
            jax.ShapeDtypeStruct((8, lines, 128), f32),
            jax.ShapeDtypeStruct((rows, 32), bf16),
            jax.ShapeDtypeStruct((32, columns), bf16),
        ),
        in_specs=[hbm] * 3,
        out_specs=(vmem,) * 6,
        scratch_shapes=[
            pltpu.VMEM(flat, f32),
            pltpu.VMEM(wall_tab.shape[1:], bf16),
            pltpu.VMEM(span_tab.shape[1:], bf16),
            pltpu.VMEM((6, slabs, 128), f32),
            pltpu.VMEM((6, lines, 128), f32),
            pltpu.VMEM((2, 3, slabs, 128), f32),
            pltpu.VMEM((2, 3, lines, 128), f32),
            pltpu.VMEM((2, max(wall_n - 2, 1), slabs, 128), f32),
            pltpu.VMEM((2, max(span_n - 2, 1), lines, 128), f32),
            pltpu.SemaphoreType.DMA((fields,)),
            pltpu.SemaphoreType.DMA((2,)),
            pltpu.SemaphoreType.DMA((2, 2, far)),
            pltpu.SemaphoreType.DMA((2, 2, far)),
        ],
        compiler_params=pltpu.CompilerParams(
            collective_id=0, has_side_effects=True, vmem_limit_bytes=43 * 1024 * 1024
        ),
        name="exchange",
    )(conserved, roomy(wall_tab), roomy(span_tab))

    group = 4
    outs = pl.pallas_call(
        functools.partial(correct_kernel, group),
        out_shape=(jax.ShapeDtypeStruct(flat, f32),) * 2,
        in_specs=[vmem] * 8,
        out_specs=(hbm, hbm),
        scratch_shapes=[
            pltpu.VMEM(flat, f32), pltpu.VMEM(flat, f32), pltpu.SemaphoreType.DMA((2, fields)),
        ],
        compiler_params=pltpu.CompilerParams(vmem_limit_bytes=24 * 1024 * 1024),
        cost_estimate=pl.CostEstimate(
            flops=2 * slabs * rows * columns * 16 * 8, bytes_accessed=8 * conserved.size, transcendentals=0
        ),
        name="correct",
    )(local[0], local[1], wall_metric, span_metric, *local[2:])
    return tuple(out.reshape(conserved.shape) for out in outs)


def solution(mesh):
    in_specs = (
        P(None, "stream", "wall", "span"),
        P("stream", "wall", "span"),
        P("stream", "wall", "span"),
    )
    out_specs = (P(None, "stream", "wall", "span"), P(None, "stream", "wall", "span"))
    sizes = (mesh.shape["wall"], mesh.shape["span"])
    return jax.shard_map(
        functools.partial(per_device, *sizes), mesh=mesh, in_specs=in_specs, out_specs=out_specs, check_vma=False
    )
```

```python
import functools

import jax
import jax.numpy as jnp
import ml_dtypes
import numpy as np
from jax import lax
from jax.experimental import pallas as pl
from jax.experimental.pallas import tpu as pltpu
from jax.sharding import PartitionSpec as P

band_alpha = 0.4995
MESH = pl.DeviceIdType.MESH


def line_operators(length_all):
    lower_band = np.full(length_all, band_alpha)
    lower_band[[1, length_all - 2]] = 0.25
    lower_band[[0, length_all - 1]] = 0.0
    band = np.eye(length_all)
    rows = np.arange(length_all)
    band[rows[1:], rows[:-1]] = lower_band[1:]
    band[rows[:-1], rows[1:]] = lower_band[:-1]
    near_coef = (band_alpha + 2.0) / 3.0
    far_coef = (4.0 * band_alpha - 1.0) / 12.0
    weights = np.zeros((5, length_all))
    weights[:, :] = np.array([-far_coef, -near_coef, 0.0, near_coef, far_coef])[:, None]
    weights[:, 1] = [0.0, -0.75, 0.0, 0.75, 0.0]
    weights[:, length_all - 2] = [0.0, -0.75, 0.0, 0.75, 0.0]
    weights[:, 0] = [0.0, 0.0, -1.5, 2.0, -0.5]
    weights[:, length_all - 1] = [0.5, -2.0, 1.5, 0.0, 0.0]
    right = np.zeros((length_all, length_all))
    for offset in range(-2, 3):
        good = rows[(rows + offset >= 0) & (rows + offset < length_all)]
        right[good, good + offset] = weights[offset + 2, good]
    inverse = np.linalg.inv(band)
    return inverse, inverse @ right


def block_tables(pieces, block):
    inverse, whole = line_operators(pieces * block)
    own = np.zeros((pieces, block, block))
    fix = np.zeros((pieces, block, 8))
    sends = np.zeros((pieces, 8, block))
    gains = np.zeros((2, pieces, max(pieces - 1, 1)))
    half = block // 2
    for p in range(pieces):
        lo, hi = p * block, (p + 1) * block
        own[p] = whole[lo:hi, lo:hi]
        sends[p, 1, block - 2] = sends[p, 2, block - 1] = 1.0
        sends[p, 4, 0] = sends[p, 5, 1] = 1.0
        if p + 1 < pieces:
            shape = inverse[hi : hi + block, hi - 1] / inverse[hi, hi - 1]
            sends[p, 0] = whole[hi + half, lo:hi] / shape[half]
            fix[p + 1, :, 0] = shape
            near = whole[hi : hi + block, hi - 2 : hi]
            fix[p + 1, :, 1:3] = near - shape[:, None] * sends[p, 0, block - 2 :]
            for d in range(1, pieces - p):
                gains[0, p + d, d - 1] = inverse[lo + d * block, hi - 1] / inverse[hi, hi - 1]
        if p > 0:
            shape = inverse[lo - block : lo, lo] / inverse[lo - 1, lo]
            sends[p, 3] = whole[lo - block + half, lo:hi] / shape[half]
            fix[p - 1, :, 3] = shape
            near = whole[lo - block : lo, lo : lo + 2]
            fix[p - 1, :, 4:6] = near - shape[:, None] * sends[p, 3, :2]
            for d in range(1, p + 1):
                gains[1, p - d, d - 1] = inverse[hi - 1 - d * block, lo] / inverse[lo - 1, lo]
    return own, fix, sends, gains


def split(table):
    high = table.astype(ml_dtypes.bfloat16)
    low = (table - high.astype(np.float64)).astype(ml_dtypes.bfloat16)
    return high, low


def roomy(table):
    pieces, rows, width = table.shape
    more = max(0, (1 << 21) // (pieces * max(width, 256)) - rows)
    return jnp.asarray(np.pad(table, ((0, 0), (0, -(-more // 16) * 16), (0, 0))))


def halves(values):
    high = values.astype(jnp.bfloat16)
    low = (values - high.astype(jnp.float32)).astype(jnp.bfloat16)
    return high, low


def exchange_kernel(
    wall_n, span_n, wall_gains, span_gains,
    f_hbm, wall_tab, span_tab,
    wall_loc, span_loc, wall_msg, span_msg, wall_fix, span_fix,
    f_buf, wall_t, span_t, wall_out, span_out, wall_near, span_near, wall_far, span_far,
    load_sems, table_sems, send_sems, recv_sems,
):
    me_w, me_s, me_c = (lax.axis_index(name) for name in ("wall", "span", "stream"))
    fields, planes, rows, columns = f_hbm.shape
    slabs = fields * planes
    loads = [
        pltpu.make_async_copy(f_hbm.at[k], f_buf.at[pl.ds(k * planes, planes)], load_sems.at[k])
        for k in range(fields)
    ]
    tables = [
        pltpu.make_async_copy(src, dst, table_sems.at[k])
        for k, (src, dst) in enumerate((
            (wall_tab.at[me_w, pl.ds(0, wall_t.shape[0])], wall_t),
            (span_tab.at[me_s, pl.ds(0, span_t.shape[0])], span_t),
        ))
    ]
    for copy in tables[:1] + loads[:2] + tables[1:] + loads[2:]:
        copy.start()

    def device(axis, shift):
        if axis == 0:
            return (me_w + shift, me_s, me_c)
        return (me_w, me_s + shift, me_c)

    axes = ((0, me_w, wall_n), (1, me_s, span_n))
    barrier = pltpu.get_barrier_semaphore()
    for axis, me, n in axes:
        for d in range(1, n):
            @pl.when(me + d < n)
            def _():
                pl.semaphore_signal(barrier, inc=1, device_id=device(axis, d), device_id_type=MESH)

            @pl.when(me >= d)
            def _():
                pl.semaphore_signal(barrier, inc=1, device_id=device(axis, -d), device_id_type=MESH)

    wall_msg[...] = jnp.zeros_like(wall_msg)
    span_msg[...] = jnp.zeros_like(span_msg)
    outs, nears, fars = (wall_out, span_out), (wall_near, span_near), (wall_far, span_far)
    gains = (wall_gains, span_gains)

    def transfer(axis, side, d):
        slot = d - 1 if d else send_sems.shape[2] - 1
        if d == 0:
            src, dst = outs[axis].at[pl.ds(3 * side + 1, 2)], nears[axis].at[side, pl.ds(1, 2)]
            d = 1
        elif d == 1:
            src, dst = outs[axis].at[3 * side], nears[axis].at[side, 0]
        else:
            src, dst = outs[axis].at[3 * side], fars[axis].at[side, d - 2]
        return pltpu.make_async_remote_copy(
            src_ref=src, dst_ref=dst,
            send_sem=send_sems.at[axis, side, slot], recv_sem=recv_sems.at[axis, side, slot],
            device_id=device(axis, d if side == 0 else -d), device_id_type=MESH,
        )

    def has_target(me, n, side, d):
        return me + max(d, 1) < n if side == 0 else me >= max(d, 1)

    def has_source(me, n, side, d):
        return me >= d if side == 0 else me + d < n

    def send_all(axis, me, n, distances):
        for d in distances:
            for side in range(2):
                @pl.when(has_target(me, n, side, d))
                def _():
                    transfer(axis, side, d).start()

    tables[0].wait()
    columns_at = 2 * rows + 32
    picks = wall_t[:rows, columns_at : columns_at + 4].astype(jnp.float32)
    picks = picks[:, :2] + picks[:, 2:]
    wall_a = jnp.broadcast_to(picks[:, 0:1], (rows, columns))
    wall_b = jnp.broadcast_to(picks[:, 1:2], (rows, columns))
    for k in range(fields):
        loads[k].wait()
        here = pl.ds(k * planes, planes)
        wall_out[1, here, :] = f_buf[here, rows - 2, :]
        wall_out[2, here, :] = f_buf[here, rows - 1, :]
        wall_out[4, here, :] = f_buf[here, 0, :]
        wall_out[5, here, :] = f_buf[here, 1, :]
    pl.semaphore_wait(barrier, wall_n + span_n - 2)
    send_all(*axes[0], (0,))
    for k in range(fields):
        here = pl.ds(k * planes, planes)
        sums = [jnp.zeros((planes, 8, columns), jnp.float32)] * 2
        for r in range(0, rows, 8):
            values = f_buf[here, r : r + 8, :]
            sums = [total + values * v[None, r : r + 8] for total, v in zip(sums, (wall_a, wall_b))]
        wall_out[0, here, :] = jnp.sum(sums[0], axis=1)
        wall_out[3, here, :] = jnp.sum(sums[1], axis=1)
    tiles = planes * rows // 128
    depth = 2 * columns
    group = 4

    def span_functionals():
        for k in range(fields):
            high, low = halves(f_buf[pl.ds(k * planes, planes)].reshape(planes * rows, columns))
            both = jnp.concatenate([high, low], axis=1)
            picked = lax.dot_general(
                span_t[depth : depth + 16], both, (((1,), (1,)), ((), ())), preferred_element_type=jnp.float32
            )
            picked = picked[:8] + picked[8:]
            for t in range(tiles):
                for m in range(6):
                    span_out[m, k * tiles + t : k * tiles + t + 1, :] = picked[m : m + 1, t * 128 : (t + 1) * 128]

    def local_products():
        @pl.loop(0, fields)
        def _(field):
            for part in range(planes // group):
                first = field * planes + part * group
                here = pl.ds(first, group)
                high, low = halves(f_buf[here])
                both = jnp.concatenate([high, low], axis=2).reshape(group * rows, depth)
                spread = jnp.dot(both, span_t[:depth], preferred_element_type=jnp.float32)
                spread = spread[:, :columns] + spread[:, columns:]
                span_loc[here] = spread.reshape(group, rows, columns)
                for q in range(0, group, 2):
                    pair = jnp.concatenate(
                        [jnp.concatenate([high[j], low[j]], axis=0) for j in (q, q + 1)], axis=1
                    )
                    solved = jnp.dot(wall_t[:, : 2 * rows], pair, preferred_element_type=jnp.float32)
                    solved = solved[:rows] + solved[rows:]
                    wall_loc[first + q] = solved[:, :columns]
                    wall_loc[first + q + 1] = solved[:, columns:]

    send_all(*axes[0], range(wall_n - 1, 0, -1))
    tables[1].wait()
    span_functionals()
    send_all(*axes[1], range(span_n - 1, -1, -1))
    local_products()

    wall_fix[...] = wall_t[:rows, 2 * rows : 2 * rows + 32]
    span_fix[...] = span_t[depth + 16 : depth + 48, :columns]

    msgs = (wall_msg, span_msg)
    for axis, me, n in axes:
        for d in range(1, n):
            for side in range(2):
                @pl.when(has_source(me, n, side, d))
                def _():
                    transfer(axis, side, d).wait_recv()
                    if d == 1:
                        transfer(axis, side, 0).wait_recv()
                    gain = jnp.float32(0.0)
                    for p in range(n):
                        gain = jnp.where(me == p, jnp.float32(gains[axis][side, p, d - 1]), gain)
                    if d == 1:
                        msgs[axis][3 * side] += gain * nears[axis][side, 0]
                        msgs[axis][3 * side + 1] = nears[axis][side, 1]
                        msgs[axis][3 * side + 2] = nears[axis][side, 2]
                    else:
                        msgs[axis][3 * side] += gain * fars[axis][side, d - 2]
    for axis, me, n in axes:
        for d in range(n):
            for side in range(2):
                @pl.when(has_target(me, n, side, d))
                def _():
                    transfer(axis, side, d).wait_send()


def correct_kernel(
    group, wall_loc, span_loc, wall_metric, span_metric, wall_msg, span_msg, wall_fix, span_fix,
    wall_hbm, span_hbm, wall_buf, span_buf, sems,
):
    planes = wall_metric.shape[0]
    slabs, rows, columns = wall_loc.shape
    tiles = group * rows // 128
    fields = slabs // planes

    def copies(field):
        here = pl.ds(field * planes, planes)
        return (
            pltpu.make_async_copy(wall_buf.at[here], wall_hbm.at[here], sems.at[0, field]),
            pltpu.make_async_copy(span_buf.at[here], span_hbm.at[here], sems.at[1, field]),
        )

    @pl.loop(0, fields)
    def _(field):
        for part in range(planes // group):
            plane = part * group
            first = field * planes + plane
            here = pl.ds(first, group)
            tile = (field * (planes // group) + part) * tiles
            edge = jnp.concatenate([span_msg[:, tile + t, :] for t in range(tiles)], axis=1)
            edge_high, edge_low = halves(edge)
            edges = [edge_high.astype(jnp.float32), edge_low.astype(jnp.float32)] * 2
            edges = jnp.concatenate(edges, axis=0).T.astype(jnp.bfloat16)
            spread = jnp.dot(edges, span_fix[...], preferred_element_type=jnp.float32)
            spread = spread.reshape(group, rows, columns)
            span_buf[here] = (span_loc[here] + spread) * span_metric[pl.ds(plane, group)]
            for q in range(0, group, 2):
                msgs = [jnp.concatenate(halves(wall_msg[:, first + j, :]) * 2, axis=0) for j in (q, q + 1)]
                solved = jnp.dot(wall_fix[...], jnp.concatenate(msgs, axis=1), preferred_element_type=jnp.float32)
                for j in range(2):
                    wall_buf[first + q + j] = (
                        wall_loc[first + q + j] + solved[:, j * columns : (j + 1) * columns]
                    ) * wall_metric[plane + q + j]
        for copy in copies(field):
            copy.start()

    @pl.loop(0, fields)
    def _(field):
        for copy in copies(field):
            copy.wait()


def per_device(wall_n, span_n, conserved, wall_metric, span_metric):
    fields, planes, rows, columns = conserved.shape
    slabs = fields * planes
    lines = slabs * rows // 128
    own_w, fix_w, sends_w, gains_w = block_tables(wall_n, rows)
    own_s, fix_s, sends_s, gains_s = block_tables(span_n, columns)
    f32, bf16 = jnp.float32, jnp.bfloat16

    own_high, own_low = split(own_w)
    fix_high, fix_low = split(fix_w)
    picks = np.concatenate(split(sends_w[:, (0, 3)].transpose(0, 2, 1)), axis=2)
    wall_tab = np.concatenate([
        np.concatenate([own_high, own_high, fix_high, fix_high, fix_low, fix_low, picks], axis=2),
        np.concatenate([own_low, own_low, fix_high, fix_high, fix_low, fix_low, picks], axis=2),
    ], axis=1)
    own_high, own_low = split(own_s.transpose(0, 2, 1))
    sends_high, sends_low = split(sends_s)
    fix_high, fix_low = split(fix_s.transpose(0, 2, 1))
    span_tab = np.concatenate(
        [np.concatenate([own_high, own_low], axis=2)] * 2
        + [np.concatenate([t, t], axis=2) for t in (sends_high, sends_low)]
        + [np.concatenate([t, t], axis=2) for t in (fix_high, fix_high, fix_low, fix_low)],
        axis=1,
    )

    vmem = pl.BlockSpec(memory_space=pltpu.VMEM)
    hbm = pl.BlockSpec(memory_space=pltpu.HBM)
    far = max(wall_n, span_n) - 1
    flat = (slabs, rows, columns)
    local = pl.pallas_call(
        functools.partial(exchange_kernel, wall_n, span_n, gains_w, gains_s),
        out_shape=(
            jax.ShapeDtypeStruct(flat, f32),
            jax.ShapeDtypeStruct(flat, f32),
            jax.ShapeDtypeStruct((8, slabs, 128), f32),
            jax.ShapeDtypeStruct((8, lines, 128), f32),
            jax.ShapeDtypeStruct((rows, 32), bf16),
            jax.ShapeDtypeStruct((32, columns), bf16),
        ),
        in_specs=[hbm] * 3,
        out_specs=(vmem,) * 6,
        scratch_shapes=[
            pltpu.VMEM(flat, f32),
            pltpu.VMEM(wall_tab.shape[1:], bf16),
            pltpu.VMEM(span_tab.shape[1:], bf16),
            pltpu.VMEM((6, slabs, 128), f32),
            pltpu.VMEM((6, lines, 128), f32),
            pltpu.VMEM((2, 3, slabs, 128), f32),
            pltpu.VMEM((2, 3, lines, 128), f32),
            pltpu.VMEM((2, max(wall_n - 2, 1), slabs, 128), f32),
            pltpu.VMEM((2, max(span_n - 2, 1), lines, 128), f32),
            pltpu.SemaphoreType.DMA((fields,)),
            pltpu.SemaphoreType.DMA((2,)),
            pltpu.SemaphoreType.DMA((2, 2, far + 1)),
            pltpu.SemaphoreType.DMA((2, 2, far + 1)),
        ],
        compiler_params=pltpu.CompilerParams(
            collective_id=0, has_side_effects=True, vmem_limit_bytes=43 * 1024 * 1024
        ),
        name="exchange",
    )(conserved, roomy(wall_tab), roomy(span_tab))

    group = 4
    outs = pl.pallas_call(
        functools.partial(correct_kernel, group),
        out_shape=(jax.ShapeDtypeStruct(flat, f32),) * 2,
        in_specs=[vmem] * 8,
        out_specs=(hbm, hbm),
        scratch_shapes=[
            pltpu.VMEM(flat, f32), pltpu.VMEM(flat, f32), pltpu.SemaphoreType.DMA((2, fields)),
        ],
        compiler_params=pltpu.CompilerParams(vmem_limit_bytes=24 * 1024 * 1024),
        cost_estimate=pl.CostEstimate(
            flops=2 * slabs * rows * columns * 16 * 8, bytes_accessed=8 * conserved.size, transcendentals=0
        ),
        name="correct",
    )(local[0], local[1], wall_metric, span_metric, *local[2:])
    return tuple(out.reshape(conserved.shape) for out in outs)


def solution(mesh):
    in_specs = (
        P(None, "stream", "wall", "span"),
        P("stream", "wall", "span"),
        P("stream", "wall", "span"),
    )
    out_specs = (P(None, "stream", "wall", "span"), P(None, "stream", "wall", "span"))
    sizes = (mesh.shape["wall"], mesh.shape["span"])
    return jax.shard_map(
        functools.partial(per_device, *sizes), mesh=mesh, in_specs=in_specs, out_specs=out_specs, check_vma=False
    )
```
